512 devices in a mesh: rows: 32 (over x, z), cols: 16 (over y, core).
Axes of the slice: x: 4, y: 8, z: 8, core: 2. Of those that a mesh axis runs over, the one named last changes fastest.
Arguments:
- matrix: float32 [65536, 4096], P('rows', 'cols'), may hold values from -80 to 80
- gaussian: float32 [256, 65536], P(None, 'rows'), may hold values from -0.046875 to 0.046875
- pivots: int32 [256], replicated, may hold values from 0 to 4095, as said below
- trailing: float32 [65536, 512], P('rows', 'cols'), may hold values from -6 to 6
Outputs:
- sketch: float32 [256, 4096], P('rows', 'cols')
- coupling: float32 [256, 512], P(None, 'cols')
- projected: float32 [65536, 512], P('rows', 'cols')
- trailing_sketch: float32 [256, 512], P('rows', 'cols')
The draws below stay inside these ranges and needn't reach their ends.
Inputs may be any that keep to these rules, and one draw needn't show every extreme that they name: `pivots`: 256 distinct column indices; at most 64 of them lie in one block of 256 consecutive columns starting at a multiple of 256, and exactly 64 in some such block.
All inputs are finite; a program needn't handle non-finite values.
Results may differ from the reference program's by a relative error of at most 0.00015.
Values sent between devices are 32-bit elements; how exact they have to be, the bound alone decides.
No kernel may reach another device: no remote copies, remote signals or barrier semaphores. Data moves between devices by JAX's collectives and lax.ppermute only.
A program may use at most 64 MiB of HBM per device.

```python
import math
import jax
import jax.numpy as jnp
from jax import lax

COLS_DEV = 256
SKETCH = 256
PANEL = 256
SLAB = 512
MOST = 64
M = 65536
N = 4096


def draw_matrix(key, part):
    key = jax.random.fold_in(key, 11)
    keys = jax.random.split(key, 3)
    position = jnp.arange(M, dtype=jnp.float32) / M
    row_scale = jnp.exp(jax.random.uniform(keys[0], (M, 1), jnp.float32, math.log(0.3), math.log(3.0)))
    row_scale = row_scale * jnp.exp(math.log(3.0) * (position - 0.5))[:, None]
    col_scale = jnp.exp(jax.random.uniform(keys[1], (1, N), jnp.float32, math.log(0.3), math.log(3.0)))
    base_values = jnp.clip(jax.random.normal(keys[2], (M, N), jnp.float32), -5.0, 5.0)
    return base_values * row_scale * col_scale


def draw_pivots(key, part):
    key = jax.random.fold_in(key, 5)
    keys = jax.random.split(key, 4)
    blocks = N // COLS_DEV
    busiest = jax.random.randint(keys[0], (), 0, blocks)
    scores = jax.random.randint(keys[1], (blocks, COLS_DEV), 0, 1 << 20) * COLS_DEV + jnp.arange(COLS_DEV)[None, :]
    ranking = jnp.argsort(scores, axis=1).astype(jnp.int32)
    busy_cols = busiest * COLS_DEV + jnp.take(ranking, busiest, axis=0)[:MOST]
    chosen = jax.random.permutation(keys[2], (blocks - 1) * MOST)[:PANEL - MOST]
    owner_block = chosen // MOST
    owner_block = owner_block + (owner_block >= busiest).astype(jnp.int32)
    other_cols = owner_block * COLS_DEV + ranking[owner_block, chosen % MOST]
    together = jnp.concatenate([busy_cols, other_cols]).astype(jnp.int32)
    return jax.random.permutation(keys[3], together).astype(jnp.int32)


def with_spikes(drawn, rng, source, target, shards_of, factor):
    owner, partner = [(jnp.arange(drawn.shape[axis_at]) // (drawn.shape[axis_at] // shards_of)).reshape([-1 if axis == axis_at else 1 for axis in range(drawn.ndim)]) for axis_at in (source, target)]
    chosen = jax.random.permutation(rng, shards_of)[partner]
    strong = (owner == chosen) | (owner == (partner + shards_of // 2) % shards_of)
    return jnp.where(strong, factor * drawn, drawn)


def block_scale(rng, extent, pieces, low, top_value):
    factor_of = 1.0
    for dim, blocks in pieces:
        steps = jax.random.uniform(jax.random.fold_in(jax.random.fold_in(rng, 6), dim), (blocks,), jnp.float32, low / len(pieces), top_value / len(pieces))
        factor_of = factor_of * jnp.repeat(jnp.exp(steps), extent[dim] // blocks).reshape((-1,) + (1,) * (len(extent) - 1 - dim))
    return factor_of


def noise(key, dims, scale, reach, cuts=(), kind=jnp.bfloat16):
    loudness = block_scale(key, dims, cuts, -0.22, 0.18) if cuts else 1.0
    result = jax.random.normal(key, dims, jnp.float32) * scale * loudness
    return jnp.minimum(jnp.maximum(result, -reach), reach).astype(kind)


def bell_draw_with(rng, extent, spread, reach, cuts, heavy, kind=jnp.bfloat16):
    array = spread * jax.random.normal(rng, extent, jnp.float32)
    if cuts:
        array = array * block_scale(rng, extent, cuts, -0.22, 0.18)
    return jnp.clip(with_spikes(array, jax.random.fold_in(rng, 3), *heavy), -reach, reach).astype(kind)


def setup_inputs(seed: int = 0) -> dict:
    streams_of = jax.random.split(jax.random.key(seed), 5)
    matrix = draw_matrix(jax.random.fold_in(streams_of[4], 71), 0)
    gaussian = bell_draw_with(streams_of[1], (SKETCH, M), M ** -0.5, 0.046875, ((1, 32),), (1, 0, 32, 2.75), jnp.float32)
    pivots = draw_pivots(jax.random.fold_in(streams_of[4], 71), 0)
    trailing = noise(streams_of[3], (M, SLAB), 1.0, 6.0, ((0, 32), (1, 16)), jnp.float32)
    return dict(matrix=matrix, gaussian=gaussian, pivots=pivots, trailing=trailing)


def inner_rows(left, right):
    return lax.dot_general(left.astype(jnp.float32), right.astype(jnp.float32), (((0,), (0,)), ((), ())), precision=lax.Precision.HIGHEST, preferred_element_type=jnp.float32)

def factor_parts(gram_matrix, cross_terms):
    chol_factor = jnp.linalg.cholesky(gram_matrix)
    coupling = lax.linalg.triangular_solve(chol_factor, cross_terms, left_side=True, lower=True)
    weights = lax.linalg.triangular_solve(chol_factor, coupling, left_side=True, lower=True, transpose_a=True)
    return (coupling, weights)

def reference(matrix, gaussian, pivots, trailing):
    highest = lax.Precision.HIGHEST
    sketch = jnp.dot(gaussian.astype(jnp.float32), matrix.astype(jnp.float32), precision=highest, preferred_element_type=jnp.float32)
    panel_block = jnp.take(matrix, pivots, axis=1)
    gram_matrix = inner_rows(panel_block, panel_block)
    cross_terms = inner_rows(panel_block, trailing)
    gauss_panel = jnp.dot(gaussian.astype(jnp.float32), panel_block.astype(jnp.float32), precision=highest, preferred_element_type=jnp.float32)
    gauss_trail = jnp.dot(gaussian.astype(jnp.float32), trailing.astype(jnp.float32), precision=highest, preferred_element_type=jnp.float32)
    coupling, weights = factor_parts(gram_matrix, cross_terms)
    projected = trailing - jnp.dot(panel_block.astype(jnp.float32), weights.astype(jnp.float32), precision=highest, preferred_element_type=jnp.float32)
    trailing_sketch = gauss_trail - jnp.dot(gauss_panel.astype(jnp.float32), weights.astype(jnp.float32), precision=highest, preferred_element_type=jnp.float32)
    return (sketch, coupling, projected, trailing_sketch)
```

```python
import jax
import jax.numpy as jnp
from jax import lax
from jax.sharding import PartitionSpec as P

MOST = 64


def inner_rows(left, right):
    return lax.dot_general(
        left,
        right,
        (((0,), (0,)), ((), ())),
        precision=lax.Precision.HIGHEST,
        preferred_element_type=jnp.float32,
    )


def product(left, right):
    return jnp.dot(left, right, precision=lax.Precision.HIGHEST, preferred_element_type=jnp.float32)


def factor_parts(gram_matrix, cross_terms):
    chol_factor = jnp.linalg.cholesky(gram_matrix)
    coupling = lax.linalg.triangular_solve(chol_factor, cross_terms, left_side=True, lower=True)
    weights = lax.linalg.triangular_solve(
        chol_factor, coupling, left_side=True, lower=True, transpose_a=True
    )
    return (coupling, weights)


def scatter_sum(partial, axis):
    n = lax.axis_size(axis)
    pieces = partial.reshape((n, partial.shape[0] // n) + partial.shape[1:])
    return jnp.sum(lax.all_to_all(pieces, axis, 0, 0, tiled=True), axis=0)


def gather_blocks(block, axis):
    n = lax.axis_size(axis)
    copies = jnp.broadcast_to(block[None], (n,) + block.shape)
    got = lax.all_to_all(copies, axis, 0, 0, tiled=True)
    return got.reshape((n * block.shape[0],) + block.shape[1:])


def shards(matrix, gaussian, pivots, trailing):
    rows_dev, cols_dev = matrix.shape
    panel_width = pivots.shape[0]
    col_groups = lax.axis_size("cols")
    col_block = lax.axis_index("cols")
    owner = pivots // cols_dev
    earlier = jnp.arange(panel_width)[None, :] < jnp.arange(panel_width)[:, None]
    slot = jnp.sum((owner[None, :] == owner[:, None]) & earlier, axis=1, dtype=jnp.int32)
    local_index = pivots - col_block * cols_dev
    column_hot = (
        lax.broadcasted_iota(jnp.int32, (cols_dev, panel_width), 0) == local_index[None, :]
    ).astype(jnp.bfloat16)
    slot_hot = (
        lax.broadcasted_iota(jnp.int32, (panel_width, MOST), 1) == slot[:, None]
    ).astype(jnp.bfloat16)
    pick = jnp.dot(column_hot, slot_hot, preferred_element_type=jnp.float32)
    mine = product(matrix, pick)
    spread = lax.all_to_all(
        mine.reshape(col_groups, rows_dev // col_groups, MOST), "cols", 0, 0, tiled=True
    )
    place = (
        lax.broadcasted_iota(jnp.int32, (col_groups * MOST, panel_width), 0)
        == (owner * MOST + slot)[None, :]
    ).astype(jnp.float32)
    part = lax.dot_general(
        spread,
        place.reshape(col_groups, MOST, panel_width),
        (((0, 2), (0, 1)), ((), ())),
        precision=lax.Precision.HIGHEST,
        preferred_element_type=jnp.float32,
    )
    panel_block = lax.all_gather(part, "cols", tiled=True)

    sketch_part = jnp.concatenate([product(gaussian, matrix), product(gaussian, trailing)], axis=1)
    sketch_rows = scatter_sum(sketch_part, "rows")
    sketch = sketch_rows[:, :cols_dev]
    gauss_trail = sketch_rows[:, cols_dev:]

    sums = scatter_sum(
        jnp.concatenate(
            [
                inner_rows(panel_block, panel_block),
                product(gaussian, panel_block),
                inner_rows(panel_block, trailing),
            ],
            axis=1,
        ),
        "rows",
    )
    gauss_panel = sums[:, panel_width : 2 * panel_width]
    whole = gather_blocks(
        jnp.concatenate([sums[:, :panel_width], sums[:, 2 * panel_width :]], axis=1), "rows"
    )
    coupling, weights = factor_parts(whole[:, :panel_width], whole[:, panel_width:])
    projected = trailing - product(panel_block, weights)
    trailing_sketch = gauss_trail - product(gauss_panel, weights)
    return (sketch, coupling, projected, trailing_sketch)


def solution(mesh):
    placed = (P("rows", "cols"), P(None, "rows"), P(), P("rows", "cols"))
    return jax.shard_map(
        shards,
        mesh=mesh,
        in_specs=placed,
        out_specs=(P("rows", "cols"), P(None, "cols"), P("rows", "cols"), P("rows", "cols")),
        check_vma=False,
    )
```

```python
import functools
import jax
import jax.numpy as jnp
from jax import lax
from jax.experimental import pallas as pl
from jax.experimental.pallas import tpu as pltpu
from jax.sharding import PartitionSpec as P

MOST = 64
BLOCK = 64
STEP = 8
LANES = 128
VMEM = pl.BlockSpec(memory_space=pltpu.VMEM)
PARAMS = pltpu.CompilerParams(vmem_limit_bytes=48 * 1024 * 1024)


def product(left, right):
    return jnp.dot(left, right, precision=lax.Precision.HIGHEST, preferred_element_type=jnp.float32)


def dot(left, right, left_dim, right_dim):
    return lax.dot_general(
        left,
        right,
        (((left_dim,), (right_dim,)), ((), ())),
        precision=lax.Precision.HIGHEST,
        preferred_element_type=jnp.float32,
    )


def hot_dot(hot, values, hot_dim, value_dim):
    high = values.astype(jnp.bfloat16)
    rest = values - high.astype(jnp.float32)
    middle = rest.astype(jnp.bfloat16)
    low = (rest - middle.astype(jnp.float32)).astype(jnp.bfloat16)
    dims = (((hot_dim,), (value_dim,)), ((), ()))
    parts = [
        lax.dot_general(hot, piece, dims, preferred_element_type=jnp.float32)
        for piece in (high, middle, low)
    ]
    return parts[0] + parts[1] + parts[2]


def dot_hot(values, hot):
    high = values.astype(jnp.bfloat16)
    rest = values - high.astype(jnp.float32)
    middle = rest.astype(jnp.bfloat16)
    low = (rest - middle.astype(jnp.float32)).astype(jnp.bfloat16)
    parts = [
        jnp.dot(piece, hot, preferred_element_type=jnp.float32) for piece in (high, middle, low)
    ]
    return parts[0] + parts[1] + parts[2]


def cost(micros):
    return pl.CostEstimate(flops=int(micros * 1e9), bytes_accessed=0, transcendentals=0)


def iota(shape, dim):
    return lax.broadcasted_iota(jnp.int32, shape, dim)


def pick_kernel(block_ref, column_ref, row_ref, matrix_ref, out_ref, pick_ref):
    width = matrix_ref.shape[1]
    count = row_ref.shape[1]

    @pl.when(pl.program_id(0) == 0)
    def _():
        row = row_ref[...]
        owner_row = row // width
        same = (column_ref[...] // width == owner_row) & (
            iota((count, count), 0) < iota((count, count), 1)
        )
        slot_row = jnp.sum(same.astype(jnp.int32), axis=0, keepdims=True)
        local_row = row - block_ref[0] * width
        by_slot = (iota((MOST, count), 0) == slot_row).astype(jnp.bfloat16)
        by_column = (iota((width, count), 0) == local_row).astype(jnp.bfloat16)
        pick_ref[...] = lax.dot_general(
            by_slot, by_column, (((1,), (1,)), ((), ())), preferred_element_type=jnp.float32
        ).astype(jnp.bfloat16)

    got = hot_dot(pick_ref[...], matrix_ref[...], 1, 1)
    for piece in range(out_ref.shape[0]):
        out_ref[piece] = got[:, piece * LANES : (piece + 1) * LANES]


def pick_columns(block, pivots, matrix, steps=4):
    rows_dev, cols_dev = matrix.shape
    count = pivots.shape[0]
    pieces = rows_dev // LANES
    return pl.pallas_call(
        pick_kernel,
        grid=(steps,),
        out_shape=jax.ShapeDtypeStruct((pieces, MOST, LANES), jnp.float32),
        in_specs=[
            pl.BlockSpec(memory_space=pltpu.SMEM),
            pl.BlockSpec((count, 1), lambda i: (0, 0)),
            pl.BlockSpec((1, count), lambda i: (0, 0)),
            pl.BlockSpec((rows_dev // steps, cols_dev), lambda i: (i, 0)),
        ],
        out_specs=pl.BlockSpec((pieces // steps, MOST, LANES), lambda i: (i, 0, 0)),
        scratch_shapes=[pltpu.VMEM((MOST, cols_dev), jnp.bfloat16)],
        compiler_params=PARAMS,
        cost_estimate=cost(2),
        name="pick_columns",
    )(block, pivots.reshape(count, 1), pivots.reshape(1, count), matrix)


def sketch_kernel(gaussian_ref, matrix_ref, slab_ref, out_ref):
    width = matrix_ref.shape[1]
    gaussian = gaussian_ref[...]
    out_ref[:, :width] = dot(gaussian, matrix_ref[...], 1, 0)
    out_ref[:, width:] = dot(gaussian, slab_ref[...], 1, 1)


def sketch_sums(gaussian, matrix, slab):
    return pl.pallas_call(
        sketch_kernel,
        out_shape=jax.ShapeDtypeStruct(
            (gaussian.shape[0], matrix.shape[1] + slab.shape[0]), jnp.float32
        ),
        in_specs=[VMEM] * 3,
        out_specs=VMEM,
        compiler_params=PARAMS,
        cost_estimate=cost(4),
        name="sketch_sums",
    )(gaussian, matrix, slab)


def part_kernel(width, column_ref, row_ref, spread_ref, sketch_ref, part_ref, send_ref):
    count = row_ref.shape[1]
    slots = spread_ref.shape[0]
    column = column_ref[...]
    owner = column // width
    same = (owner == row_ref[...] // width) & (iota((count, count), 1) < iota((count, count), 0))
    slot = jnp.sum(same.astype(jnp.int32), axis=1, keepdims=True)
    place = (iota((count, slots), 1) == owner * MOST + slot).astype(jnp.bfloat16)
    part = hot_dot(place, spread_ref[...], 1, 0)
    part_ref[...] = part
    send_ref[:, :, :count] = dot(part, part, 1, 1).reshape(send_ref.shape[0], -1, count)
    send_ref[:, :, count:] = sketch_ref[...]


def part_products(width, pivots, spread, sketch):
    count = pivots.shape[0]
    pieces, rows, lanes = sketch.shape
    return pl.pallas_call(
        functools.partial(part_kernel, width),
        out_shape=(
            jax.ShapeDtypeStruct((count, LANES), jnp.float32),
            jax.ShapeDtypeStruct((pieces, rows, count + lanes), jnp.float32),
        ),
        in_specs=[VMEM] * 4,
        out_specs=(VMEM,) * 2,
        compiler_params=PARAMS,
        cost_estimate=cost(2),
        name="part_products",
    )(pivots.reshape(count, 1), pivots.reshape(1, count), spread, sketch)


def row_sums_kernel(block_ref, row_ref, got_ref, send_ref, sketch_ref, trail_ref):
    width = sketch_ref.shape[1]
    count = row_ref.shape[1]
    total = jnp.sum(got_ref[...], axis=0)
    sketch = total[:, count : count + width]
    sketch_ref[...] = sketch
    trail_ref[...] = total[:, count + width :]
    local_row = row_ref[...] - block_ref[0] * width
    by_column = (iota((width, count), 0) == local_row).astype(jnp.bfloat16)
    both = jnp.concatenate([total[:, :count], dot_hot(sketch, by_column)], axis=1)
    for piece in range(send_ref.shape[0]):
        send_ref[piece] = both


def row_sums(block, pivots, got, width, pieces):
    count = pivots.shape[0]
    _, rows, lanes = got.shape
    return pl.pallas_call(
        row_sums_kernel,
        out_shape=(
            jax.ShapeDtypeStruct((pieces, rows, 2 * count), jnp.float32),
            jax.ShapeDtypeStruct((rows, width), jnp.float32),
            jax.ShapeDtypeStruct((rows, lanes - count - width), jnp.float32),
        ),
        in_specs=[pl.BlockSpec(memory_space=pltpu.SMEM), VMEM, VMEM],
        out_specs=(VMEM,) * 3,
        compiler_params=PARAMS,
        cost_estimate=cost(1),
        name="row_sums",
    )(block, pivots.reshape(1, count), got)


def col_sums_kernel(got_ref, panel_ref, slab_ref, send_ref, gauss_ref):
    total = jnp.sum(got_ref[...], axis=0)
    count = gauss_ref.shape[1]
    gauss_ref[...] = total[:, count:]
    rows = total.shape[0]
    cross = jnp.zeros((count, slab_ref.shape[0]), jnp.float32)
    for piece in range(panel_ref.shape[0]):
        at = slice(piece * LANES, (piece + 1) * LANES)
        cross += dot(panel_ref[piece], slab_ref[:, at], 1, 1)
    for piece in range(send_ref.shape[0]):
        send_ref[piece, :, :count] = total[:, :count]
        send_ref[piece, :, count:] = cross[piece * rows : (piece + 1) * rows]


def col_sums(got, panel, slab, pieces):
    _, rows, both = got.shape
    count = both // 2
    return pl.pallas_call(
        col_sums_kernel,
        out_shape=(
            jax.ShapeDtypeStruct((pieces, rows, count + slab.shape[0]), jnp.float32),
            jax.ShapeDtypeStruct((rows, count), jnp.float32),
        ),
        in_specs=[VMEM] * 3,
        out_specs=(VMEM,) * 2,
        compiler_params=PARAMS,
        cost_estimate=cost(2),
        name="col_sums",
    )(got, panel, slab)


def cross_sums_kernel(got_ref, send_ref):
    count = got_ref.shape[2] - send_ref.shape[2]
    total = jnp.sum(got_ref[:, :, count:], axis=0)
    for piece in range(send_ref.shape[0]):
        send_ref[piece] = total


def cross_sums(got, slab_cols):
    pieces, rows, _ = got.shape
    return pl.pallas_call(
        cross_sums_kernel,
        out_shape=jax.ShapeDtypeStruct((pieces, rows, slab_cols), jnp.float32),
        in_specs=[VMEM],
        out_specs=VMEM,
        compiler_params=PARAMS,
        cost_estimate=cost(1),
        name="cross_sums",
    )(got)


def block_inverse(block):
    n = block.shape[0]
    groups = n // 8
    sub = iota((8, 2 * n), 0)
    eye = (iota((n, n), 0) == iota((n, n), 1)).astype(jnp.float32)
    whole = jnp.concatenate([block, eye], axis=1)
    rows = [whole[8 * g : 8 * g + 8] for g in range(groups)]
    diag = [jnp.ones((8, 2 * n), jnp.float32) for _ in rows]
    for first in range(0, n, STEP):
        cols = [
            {
                g: jnp.broadcast_to(rows[g][:, j : j + 1], (8, 2 * n))
                for g in range(first // 8, groups)
            }
            for j in range(first, first + STEP)
        ]
        for t in range(STEP):
            k = first + t
            at, s = k // 8, k % 8
            col = cols[t]
            pivot = jnp.broadcast_to(col[at][s : s + 1], (8, 2 * n))
            inverse = 1.0 / pivot
            diag[at] = jnp.where(sub == s, pivot, diag[at])
            scaled = jnp.broadcast_to(rows[at][s : s + 1], (8, 2 * n)) * inverse
            for u in range(t + 1, STEP):
                other = jnp.broadcast_to(cols[u][at][s : s + 1], (8, 2 * n)) * inverse
                for g in range(at, groups):
                    cols[u][g] = cols[u][g] - col[g] * other
            for g in range(at, groups):
                factor = col[g] if g > at else jnp.where(sub > s, col[g], 0.0)
                rows[g] = rows[g] - factor * scaled
    out = jnp.concatenate([r * lax.rsqrt(d) for r, d in zip(rows, diag)], axis=0)
    return out[:, n:]


def inverse_kernel(gram_ref, out_ref, work):
    n = out_ref.shape[0]
    work[:, :n] = gram_ref[:, :, :n].reshape(n, n)
    work[:, n:] = (iota((n, n), 0) == iota((n, n), 1)).astype(jnp.float32)
    for top in range(0, n, BLOCK):
        end = top + BLOCK
        inv = block_inverse(work[top:end, top:end])
        if end == n:
            out_ref[top:end, :] = dot(inv, work[top:end, n:], 1, 0)
            break
        lo = end // LANES * LANES
        hi = -(-(n + end) // LANES) * LANES
        strip = dot(inv, work[top:end, lo:hi], 1, 0)
        done = strip[:, n - lo :]
        if hi < 2 * n:
            done = jnp.concatenate([done, jnp.zeros((BLOCK, 2 * n - hi), jnp.float32)], axis=1)
        out_ref[top:end, :] = done
        work[end:, lo:hi] -= dot(strip[:, end - lo : n - lo], strip, 0, 0)


def inverse_factor(gram):
    n = gram.shape[0] * gram.shape[1]
    return pl.pallas_call(
        inverse_kernel,
        out_shape=jax.ShapeDtypeStruct((n, n), jnp.float32),
        in_specs=[VMEM],
        out_specs=VMEM,
        scratch_shapes=[pltpu.VMEM((n, 2 * n), jnp.float32)],
        compiler_params=PARAMS,
        cost_estimate=cost(10),
        name="inverse_factor",
    )(gram)


def finish_kernel(inv_ref, cross_ref, panel_ref, slab_ref, gauss_ref, trail_ref, coupling_ref, projected_ref, sketch_ref):
    inv = inv_ref[...]
    coupling = dot(cross_ref[...], inv, 0, 1)
    coupling_ref[...] = coupling
    weights = dot(coupling, inv, 1, 0)
    for piece in range(panel_ref.shape[0]):
        at = slice(piece * LANES, (piece + 1) * LANES)
        projected_ref[:, at] = slab_ref[:, at] - dot(weights, panel_ref[piece], 1, 0)
    sketch_ref[...] = trail_ref[...] - dot(gauss_ref[...], weights, 1, 1)


def finish(inv, cross, panel, slab, gauss_panel, gauss_trail):
    return pl.pallas_call(
        finish_kernel,
        out_shape=(
            jax.ShapeDtypeStruct(cross.shape[::-1], jnp.float32),
            jax.ShapeDtypeStruct(slab.shape, jnp.float32),
            jax.ShapeDtypeStruct(gauss_trail.shape, jnp.float32),
        ),
        in_specs=[VMEM] * 6,
        out_specs=(VMEM,) * 3,
        compiler_params=PARAMS,
        cost_estimate=cost(3),
        name="finish",
    )(inv, cross, panel, slab, gauss_panel, gauss_trail)


def exchange(pieces, axis):
    return lax.all_to_all(pieces, axis, 0, 0, tiled=True)


def shards(matrix, gaussian, pivots, trailing):
    rows_dev, cols_dev = matrix.shape
    count = pivots.shape[0]
    slab_cols = trailing.shape[1]
    n_rows = lax.axis_size("rows")
    n_cols = lax.axis_size("cols")
    block = lax.axis_index("cols").reshape(1)
    slab = trailing.T

    mine = pick_columns(block, pivots, matrix)
    spread = exchange(mine, "cols")
    late_gaussian, mine = lax.optimization_barrier((gaussian, mine))
    sketch_part = sketch_sums(late_gaussian, matrix, slab)

    part, send = part_products(
        cols_dev,
        pivots,
        spread.reshape(n_cols * MOST, LANES),
        sketch_part.reshape(n_rows, -1, cols_dev + slab_cols),
    )
    panel = lax.all_gather(part, "cols")
    send, sketch, gauss_trail = row_sums(block, pivots, exchange(send, "rows"), cols_dev, n_cols)
    send, gauss_panel = col_sums(exchange(send, "cols"), panel, slab, n_rows)
    got = exchange(send, "rows")
    cross = exchange(cross_sums(got, slab_cols), "rows").reshape(count, slab_cols)
    inv = inverse_factor(got)
    coupling, projected, trailing_sketch = finish(
        inv, cross, panel, slab, gauss_panel, gauss_trail
    )
    return (sketch, coupling.T, projected.T, trailing_sketch)


def solution(mesh):
    placed = (P("rows", "cols"), P(None, "rows"), P(), P("rows", "cols"))
    return jax.shard_map(
        shards,
        mesh=mesh,
        in_specs=placed,
        out_specs=(P("rows", "cols"), P(None, "cols"), P("rows", "cols"), P("rows", "cols")),
        check_vma=False,
    )
```

```python
import functools
import jax
import jax.numpy as jnp
from jax import lax
from jax.experimental import pallas as pl
from jax.experimental.pallas import tpu as pltpu
from jax.sharding import PartitionSpec as P

MOST = 64
BLOCK = 64
STEP = 8
LANES = 128
VMEM = pl.BlockSpec(memory_space=pltpu.VMEM)
HBM = pl.BlockSpec(memory_space=pltpu.HBM)
PARAMS = pltpu.CompilerParams(vmem_limit_bytes=48 * 1024 * 1024)
FETCHING = pltpu.CompilerParams(vmem_limit_bytes=60 * 1024 * 1024)


def product(left, right):
    return jnp.dot(left, right, precision=lax.Precision.HIGHEST, preferred_element_type=jnp.float32)


def dot(left, right, left_dim, right_dim):
    return lax.dot_general(
        left,
        right,
        (((left_dim,), (right_dim,)), ((), ())),
        precision=lax.Precision.HIGHEST,
        preferred_element_type=jnp.float32,
    )


def hot_dot(hot, values, hot_dim, value_dim):
    high = values.astype(jnp.bfloat16)
    rest = values - high.astype(jnp.float32)
    middle = rest.astype(jnp.bfloat16)
    low = (rest - middle.astype(jnp.float32)).astype(jnp.bfloat16)
    dims = (((hot_dim,), (value_dim,)), ((), ()))
    parts = [
        lax.dot_general(hot, piece, dims, preferred_element_type=jnp.float32)
        for piece in (high, middle, low)
    ]
    return parts[0] + parts[1] + parts[2]


def dot_hot(values, hot):
    high = values.astype(jnp.bfloat16)
    rest = values - high.astype(jnp.float32)
    middle = rest.astype(jnp.bfloat16)
    low = (rest - middle.astype(jnp.float32)).astype(jnp.bfloat16)
    parts = [
        jnp.dot(piece, hot, preferred_element_type=jnp.float32) for piece in (high, middle, low)
    ]
    return parts[0] + parts[1] + parts[2]


def cost(micros):
    return pl.CostEstimate(flops=int(micros * 1e9), bytes_accessed=0, transcendentals=0)


def iota(shape, dim):
    return lax.broadcasted_iota(jnp.int32, shape, dim)


def pack_slab(ref, cols):
    per = LANES // cols
    rows = ref.shape[0] // per
    return jnp.concatenate(
        [ref[pl.ds(p, rows, stride=per), :][:, :cols] for p in range(per)], axis=1
    )


def unpack_slab(ref, packed, cols):
    per = LANES // cols
    rows = packed.shape[0]
    for p in range(per):
        piece = jnp.concatenate(
            [packed[:, p * cols : (p + 1) * cols], jnp.zeros((rows, LANES - cols), jnp.float32)],
            axis=1,
        )
        ref[pl.ds(p, rows, stride=per), :] = piece


def pick_kernel(block_ref, row_hbm, matrix_hbm, out_ref, row_ref, matrix_ref, row_sem, sems):
    steps = sems.shape[0]
    rows, width = matrix_ref.shape
    count = row_ref.shape[1]
    chunk = rows // steps
    fetch_row = pltpu.make_async_copy(row_hbm, row_ref, row_sem)
    fetch_row.start()
    fetches = []
    for i in range(steps):
        at = pl.ds(i * chunk, chunk)
        fetch = pltpu.make_async_copy(matrix_hbm.at[at, :], matrix_ref.at[at, :], sems.at[i])
        fetch.start()
        fetches.append(fetch)
    fetch_row.wait()
    row = row_ref[...]
    owner_row = row // width
    diagonal = iota((count, count), 0) == iota((count, count), 1)
    owner_column = jnp.sum(jnp.where(diagonal, owner_row, 0), axis=1, keepdims=True)
    same = (owner_column == owner_row) & (iota((count, count), 0) < iota((count, count), 1))
    slot_row = jnp.sum(same.astype(jnp.int32), axis=0, keepdims=True)
    local_row = row - block_ref[0] * width
    by_slot = (iota((MOST, count), 0) == slot_row).astype(jnp.bfloat16)
    by_column = (iota((width, count), 0) == local_row).astype(jnp.bfloat16)
    pick = lax.dot_general(
        by_slot, by_column, (((1,), (1,)), ((), ())), preferred_element_type=jnp.float32
    ).astype(jnp.bfloat16)
    for i in range(steps):
        fetches[i].wait()
        got = hot_dot(pick, matrix_ref[i * chunk : (i + 1) * chunk, :], 1, 1)
        for piece in range(chunk // LANES):
            out_ref[i * (chunk // LANES) + piece] = got[:, piece * LANES : (piece + 1) * LANES]


def pick_columns(block, pivots, matrix, steps=2):
    rows_dev, cols_dev = matrix.shape
    count = pivots.shape[0]
    return pl.pallas_call(
        pick_kernel,
        out_shape=jax.ShapeDtypeStruct((rows_dev // LANES, MOST, LANES), jnp.float32),
        in_specs=[pl.BlockSpec(memory_space=pltpu.SMEM), HBM, HBM],
        out_specs=VMEM,
        scratch_shapes=[
            pltpu.VMEM((1, count), jnp.int32),
            pltpu.VMEM((rows_dev, cols_dev), jnp.float32),
            pltpu.SemaphoreType.DMA,
            pltpu.SemaphoreType.DMA((steps,)),
        ],
        compiler_params=FETCHING,
        cost_estimate=cost(2),
        name="pick_columns",
    )(block, pivots.reshape(1, count), matrix)


def sketch_kernel(gaussian_ref, matrix_ref, slab_ref, out_ref, trail_ref):
    pieces = out_ref.shape[0]
    width = matrix_ref.shape[1]
    cols = slab_ref.shape[0]
    gaussian = gaussian_ref[...]
    sketch = dot(gaussian, matrix_ref[...], 1, 0)
    for half in range(width // LANES):
        out_ref[:, 8 * half : 8 * half + 8, :] = sketch[
            :, half * LANES : (half + 1) * LANES
        ].reshape(pieces, 8, LANES)
    trail_ref[:, :cols] = dot(gaussian, slab_ref[...], 1, 1)
    packed = pack_slab(trail_ref, cols)
    at = 8 * (width // LANES)
    for piece in range(pieces):
        out_ref[piece, at : at + 2, :] = packed[2 * piece : 2 * piece + 2]
        out_ref[piece, at + 2 :, :] = jnp.zeros((6, LANES), jnp.float32)


def sketch_sums(gaussian, matrix, slab, pieces):
    return pl.pallas_call(
        sketch_kernel,
        out_shape=jax.ShapeDtypeStruct((pieces, 24, LANES), jnp.float32),
        in_specs=[VMEM] * 3,
        out_specs=VMEM,
        scratch_shapes=[pltpu.VMEM((gaussian.shape[0], LANES), jnp.float32)],
        compiler_params=PARAMS,
        cost_estimate=cost(4),
        name="sketch_sums",
    )(gaussian, matrix, slab)


def part_kernel(width, row_ref, spread_ref, part_ref):
    count = row_ref.shape[1]
    slots = spread_ref.shape[0]
    owner_row = row_ref[...] // width
    diagonal = iota((count, count), 0) == iota((count, count), 1)
    owner = jnp.sum(jnp.where(diagonal, owner_row, 0), axis=1, keepdims=True)
    same = (owner == owner_row) & (iota((count, count), 1) < iota((count, count), 0))
    slot = jnp.sum(same.astype(jnp.int32), axis=1, keepdims=True)
    place = (iota((count, slots), 1) == owner * MOST + slot).astype(jnp.bfloat16)
    part_ref[...] = hot_dot(place, spread_ref[...], 1, 0)


def panel_part(width, pivots, spread):
    count = pivots.shape[0]
    return pl.pallas_call(
        functools.partial(part_kernel, width),
        out_shape=jax.ShapeDtypeStruct((count, LANES), jnp.float32),
        in_specs=[VMEM, VMEM],
        out_specs=VMEM,
        compiler_params=PARAMS,
        cost_estimate=cost(1),
        name="panel_part",
    )(pivots.reshape(1, count), spread)


def gram_kernel(part_ref, sketch_ref, send_ref, gram_ref):
    half = part_ref.shape[0] // 2
    gram_ref[...] = dot(part_ref[...], part_ref[...], 1, 1)
    send_ref[:, 0:16, :] = sketch_ref[:, 0:16, :]
    send_ref[:, 28:32, :] = sketch_ref[:, 16:20, :]
    for piece in range(send_ref.shape[0]):
        low = 4 * piece
        send_ref[piece, 16:20, :] = gram_ref[low : low + 4, :half]
        send_ref[piece, 20:24, :] = gram_ref[low : low + 4, half:]
        send_ref[piece, 24:28, :] = gram_ref[half + low : half + low + 4, half:]


def gram_products(part, sketch):
    count = part.shape[0]
    pieces = sketch.shape[0]
    return pl.pallas_call(
        gram_kernel,
        out_shape=jax.ShapeDtypeStruct((pieces, 32, LANES), jnp.float32),
        in_specs=[VMEM, VMEM],
        out_specs=VMEM,
        scratch_shapes=[pltpu.VMEM((count, count), jnp.float32)],
        compiler_params=PARAMS,
        cost_estimate=cost(1),
        name="gram_products",
    )(part, sketch)


def row_sums_kernel(block_ref, row_ref, got_ref, send_ref, sketch_ref, trail_ref):
    width = sketch_ref.shape[1]
    count = row_ref.shape[1]
    total = jnp.sum(got_ref[...], axis=0)
    sketch = jnp.concatenate([total[0:8], total[8:16]], axis=1)
    sketch_ref[...] = sketch
    trail_ref[...] = total[28:30]
    local_row = row_ref[...] - block_ref[0] * width
    by_column = (iota((width, count), 0) == local_row).astype(jnp.bfloat16)
    chosen = dot_hot(sketch, by_column)
    both = jnp.concatenate([chosen[:, :LANES], chosen[:, LANES:], total[16:32]], axis=0)
    for piece in range(send_ref.shape[0]):
        send_ref[piece] = both


def row_sums(block, pivots, got, width, pieces):
    count = pivots.shape[0]
    return pl.pallas_call(
        row_sums_kernel,
        out_shape=(
            jax.ShapeDtypeStruct((pieces, 32, LANES), jnp.float32),
            jax.ShapeDtypeStruct((8, width), jnp.float32),
            jax.ShapeDtypeStruct((2, LANES), jnp.float32),
        ),
        in_specs=[pl.BlockSpec(memory_space=pltpu.SMEM), VMEM, VMEM],
        out_specs=(VMEM,) * 3,
        compiler_params=PARAMS,
        cost_estimate=cost(1),
        name="row_sums",
    )(block, pivots.reshape(1, count), got)


def col_sums_kernel(got_ref, panel_ref, slab_ref, send_ref, gauss_ref, cross_ref):
    cols = slab_ref.shape[0]
    pieces = send_ref.shape[0]
    panel = jnp.concatenate([panel_ref[k] for k in range(panel_ref.shape[0])], axis=1)
    cross_ref[:, :cols] = dot(panel, slab_ref[...], 1, 1)
    total = jnp.sum(got_ref[...], axis=0)
    gauss_ref[...] = jnp.concatenate([total[0:8], total[8:16]], axis=1)
    gram = total[16:28]
    packed = pack_slab(cross_ref, cols)
    for piece in range(pieces):
        send_ref[piece, 0:12, :] = gram
        send_ref[piece, 12:14, :] = packed[2 * piece : 2 * piece + 2]
        send_ref[piece, 14:16, :] = jnp.zeros((2, LANES), jnp.float32)


def col_sums(got, panel, slab, pieces):
    count = panel.shape[1]
    return pl.pallas_call(
        col_sums_kernel,
        out_shape=(
            jax.ShapeDtypeStruct((pieces, 16, LANES), jnp.float32),
            jax.ShapeDtypeStruct((8, count), jnp.float32),
        ),
        in_specs=[VMEM] * 3,
        out_specs=(VMEM,) * 2,
        scratch_shapes=[pltpu.VMEM((count, LANES), jnp.float32)],
        compiler_params=PARAMS,
        cost_estimate=cost(2),
        name="col_sums",
    )(got, panel, slab)


def cross_sums_kernel(got_ref, send_ref):
    total = jnp.sum(got_ref[:, 8:16, :], axis=0)[4:6]
    for piece in range(send_ref.shape[0]):
        send_ref[piece] = total


def cross_sums(got):
    pieces = got.shape[0]
    return pl.pallas_call(
        cross_sums_kernel,
        out_shape=jax.ShapeDtypeStruct((pieces, 2, LANES), jnp.float32),
        in_specs=[VMEM],
        out_specs=VMEM,
        compiler_params=PARAMS,
        cost_estimate=cost(1),
        name="cross_sums",
    )(got)


def block_inverse(block):
    n = block.shape[0]
    groups = n // 8
    sub = iota((8, 2 * n), 0)
    eye = (iota((n, n), 0) == iota((n, n), 1)).astype(jnp.float32)
    whole = jnp.concatenate([block, eye], axis=1)
    rows = [whole[8 * g : 8 * g + 8] for g in range(groups)]
    diag = [jnp.ones((8, 2 * n), jnp.float32) for _ in rows]
    for first in range(0, n, STEP):
        cols = [
            {
                g: jnp.broadcast_to(rows[g][:, j : j + 1], (8, 2 * n))
                for g in range(first // 8, groups)
            }
            for j in range(first, first + STEP)
        ]
        for t in range(STEP):
            k = first + t
            at, s = k // 8, k % 8
            col = cols[t]
            pivot = jnp.broadcast_to(col[at][s : s + 1], (8, 2 * n))
            inverse = 1.0 / pivot
            diag[at] = jnp.where(sub == s, pivot, diag[at])
            scaled = jnp.broadcast_to(rows[at][s : s + 1], (8, 2 * n)) * inverse
            for u in range(t + 1, STEP):
                other = jnp.broadcast_to(cols[u][at][s : s + 1], (8, 2 * n)) * inverse
                for g in range(at, groups):
                    cols[u][g] = cols[u][g] - col[g] * other
            for g in range(at, groups):
                factor = col[g] if g > at else jnp.where(sub > s, col[g], 0.0)
                rows[g] = rows[g] - factor * scaled
    out = jnp.concatenate([r * lax.rsqrt(d) for r, d in zip(rows, diag)], axis=0)
    return out[:, n:]


def inverse_kernel(gram_ref, out_ref, work):
    n = out_ref.shape[0]
    half = n // 2
    for piece in range(gram_ref.shape[0]):
        low = 4 * piece
        work[low : low + 4, :half] = gram_ref[piece, 0:4, :]
        work[low : low + 4, half:n] = gram_ref[piece, 4:8, :]
        work[half + low : half + low + 4, half:n] = gram_ref[piece, 8:12, :]
    work[half:, :half] = jnp.zeros((half, half), jnp.float32)
    work[:, n:] = (iota((n, n), 0) == iota((n, n), 1)).astype(jnp.float32)
    for top in range(0, n, BLOCK):
        end = top + BLOCK
        inv = block_inverse(work[top:end, top:end])
        if end == n:
            out_ref[top:end, :] = dot(inv, work[top:end, n:], 1, 0)
            break
        lo = end // LANES * LANES
        hi = -(-(n + end) // LANES) * LANES
        strip = dot(inv, work[top:end, lo:hi], 1, 0)
        done = strip[:, n - lo :]
        if hi < 2 * n:
            done = jnp.concatenate([done, jnp.zeros((BLOCK, 2 * n - hi), jnp.float32)], axis=1)
        out_ref[top:end, :] = done
        work[end:, lo:hi] -= dot(strip[:, end - lo : n - lo], strip, 0, 0)


def inverse_factor(gram, n):
    return pl.pallas_call(
        inverse_kernel,
        out_shape=jax.ShapeDtypeStruct((n, n), jnp.float32),
        in_specs=[VMEM],
        out_specs=VMEM,
        scratch_shapes=[pltpu.VMEM((n, 2 * n), jnp.float32)],
        compiler_params=PARAMS,
        cost_estimate=cost(10),
        name="inverse_factor",
    )(gram)


def finish_kernel(inv_ref, packed_ref, panel_ref, slab_ref, gauss_ref, trail_ref, coupling_ref, projected_ref, sketch_ref, cross_ref):
    cols = slab_ref.shape[0]
    inv = inv_ref[...]
    unpack_slab(cross_ref, packed_ref[...], cols)
    coupling = dot(cross_ref[:, :cols], inv, 0, 1)
    coupling_ref[...] = coupling
    weights = dot(coupling, inv, 1, 0)
    group = panel_ref.shape[0] // 2
    for low in range(0, panel_ref.shape[0], group):
        at = slice(low * LANES, (low + group) * LANES)
        panel = jnp.concatenate([panel_ref[k] for k in range(low, low + group)], axis=1)
        projected_ref[:, at] = slab_ref[:, at] - dot(weights, panel, 1, 0)
    per = LANES // cols
    trail = jnp.concatenate(
        [
            trail_ref[m : m + 1, p * cols : (p + 1) * cols]
            for m in range(trail_ref.shape[0])
            for p in range(per)
        ],
        axis=0,
    )
    sketch_ref[...] = trail - dot(gauss_ref[...], weights, 1, 1)


def finish(inv, cross, panel, slab, gauss_panel, gauss_trail):
    count = panel.shape[1]
    cols = slab.shape[0]
    return pl.pallas_call(
        finish_kernel,
        out_shape=(
            jax.ShapeDtypeStruct((cols, count), jnp.float32),
            jax.ShapeDtypeStruct(slab.shape, jnp.float32),
            jax.ShapeDtypeStruct((gauss_panel.shape[0], cols), jnp.float32),
        ),
        in_specs=[VMEM] * 6,
        out_specs=(VMEM,) * 3,
        scratch_shapes=[pltpu.VMEM((count, LANES), jnp.float32)],
        compiler_params=PARAMS,
        cost_estimate=cost(3),
        name="finish",
    )(inv, cross, panel, slab, gauss_panel, gauss_trail)


def exchange(pieces, axis):
    return lax.all_to_all(pieces, axis, 0, 0, tiled=True)


def shards(matrix, gaussian, pivots, trailing):
    rows_dev, cols_dev = matrix.shape
    count = pivots.shape[0]
    slab_cols = trailing.shape[1]
    n_rows = lax.axis_size("rows")
    n_cols = lax.axis_size("cols")
    block = lax.axis_index("cols").reshape(1)
    slab = trailing.T

    mine = pick_columns(block, pivots, matrix)
    spread = exchange(mine, "cols")
    late_gaussian, mine = lax.optimization_barrier((gaussian, mine))
    sketch_part = sketch_sums(late_gaussian, matrix, slab, n_rows)

    spread, sketch_part = lax.optimization_barrier((spread, sketch_part))
    part = panel_part(cols_dev, pivots, spread.reshape(n_cols * MOST, LANES))
    panel = lax.all_gather(part, "cols")
    send = gram_products(part, sketch_part)
    send, sketch, gauss_trail = row_sums(block, pivots, exchange(send, "rows"), cols_dev, n_cols)
    send, gauss_panel = col_sums(exchange(send, "cols"), panel, slab, n_rows)
    got = exchange(send, "rows")
    cross = exchange(cross_sums(got), "rows").reshape(-1, LANES)
    inv = inverse_factor(got, count)
    coupling, projected, trailing_sketch = finish(
        inv, cross, panel, slab, gauss_panel, gauss_trail
    )
    return (sketch, coupling.T, projected.T, trailing_sketch)


def solution(mesh):
    placed = (P("rows", "cols"), P(None, "rows"), P(), P("rows", "cols"))
    return jax.shard_map(
        shards,
        mesh=mesh,
        in_specs=placed,
        out_specs=(P("rows", "cols"), P(None, "cols"), P("rows", "cols"), P("rows", "cols")),
        check_vma=False,
    )
```

```python
import functools
import jax
import jax.numpy as jnp
from jax import lax
from jax.experimental import pallas as pl
from jax.experimental.pallas import tpu as pltpu
from jax.sharding import PartitionSpec as P

MOST = 64
BLOCK = 64
STEP = 16
LANES = 128
HOPS = (0, 7, 6, 5, 4, 1, 2, 3)
VMEM = pl.BlockSpec(memory_space=pltpu.VMEM)
HBM = pl.BlockSpec(memory_space=pltpu.HBM)
PARAMS = pltpu.CompilerParams(vmem_limit_bytes=48 * 1024 * 1024)
FETCHING = pltpu.CompilerParams(vmem_limit_bytes=60 * 1024 * 1024)


def product(left, right):
    return jnp.dot(left, right, precision=lax.Precision.HIGHEST, preferred_element_type=jnp.float32)


def dot(left, right, left_dim, right_dim):
    return lax.dot_general(
        left,
        right,
        (((left_dim,), (right_dim,)), ((), ())),
        precision=lax.Precision.HIGHEST,
        preferred_element_type=jnp.float32,
    )


def hot_dot(hot, values, hot_dim, value_dim):
    high = values.astype(jnp.bfloat16)
    rest = values - high.astype(jnp.float32)
    middle = rest.astype(jnp.bfloat16)
    low = (rest - middle.astype(jnp.float32)).astype(jnp.bfloat16)
    dims = (((hot_dim,), (value_dim,)), ((), ()))
    parts = [
        lax.dot_general(hot, piece, dims, preferred_element_type=jnp.float32)
        for piece in (high, middle, low)
    ]
    return parts[0] + parts[1] + parts[2]


def dot_hot(values, hot):
    high = values.astype(jnp.bfloat16)
    rest = values - high.astype(jnp.float32)
    middle = rest.astype(jnp.bfloat16)
    low = (rest - middle.astype(jnp.float32)).astype(jnp.bfloat16)
    parts = [
        jnp.dot(piece, hot, preferred_element_type=jnp.float32) for piece in (high, middle, low)
    ]
    return parts[0] + parts[1] + parts[2]


def cost(micros):
    return pl.CostEstimate(flops=int(micros * 1e9), bytes_accessed=0, transcendentals=0)


def iota(shape, dim):
    return lax.broadcasted_iota(jnp.int32, shape, dim)


def pack_slab(ref, cols):
    per = LANES // cols
    rows = ref.shape[0] // per
    return jnp.concatenate(
        [ref[pl.ds(p, rows, stride=per), :][:, :cols] for p in range(per)], axis=1
    )


def pick_kernel(block_ref, row_hbm, matrix_hbm, slab_hbm, out_ref, row_ref, matrix_ref, slab_ref, row_sem, slab_sem, sems):
    steps = sems.shape[0]
    rows, width = matrix_ref.shape
    count = row_ref.shape[1]
    chunk = rows // steps
    fetch_row = pltpu.make_async_copy(row_hbm, row_ref, row_sem)
    fetch_row.start()
    fetches = []
    for i in range(steps):
        at = pl.ds(i * chunk, chunk)
        fetch = pltpu.make_async_copy(matrix_hbm.at[at, :], matrix_ref.at[at, :], sems.at[i])
        fetch.start()
        fetches.append(fetch)
    fetch_slab = pltpu.make_async_copy(slab_hbm, slab_ref, slab_sem)
    fetch_slab.start()
    fetch_row.wait()
    row = row_ref[...]
    owner_row = row // width
    diagonal = iota((count, count), 0) == iota((count, count), 1)
    owner_column = jnp.sum(jnp.where(diagonal, owner_row, 0), axis=1, keepdims=True)
    same = (owner_column == owner_row) & (iota((count, count), 0) < iota((count, count), 1))
    slot_row = jnp.sum(same.astype(jnp.int32), axis=0, keepdims=True)
    local_row = row - block_ref[0] * width
    by_slot = (iota((MOST, count), 0) == slot_row).astype(jnp.bfloat16)
    by_column = (iota((width, count), 0) == local_row).astype(jnp.bfloat16)
    pick = lax.dot_general(
        by_slot, by_column, (((1,), (1,)), ((), ())), preferred_element_type=jnp.float32
    ).astype(jnp.bfloat16)
    for i in range(steps):
        fetches[i].wait()
        got = hot_dot(pick, matrix_ref[i * chunk : (i + 1) * chunk, :], 1, 1)
        for piece in range(chunk // LANES):
            out_ref[i * (chunk // LANES) + piece, :MOST, :] = got[
                :, piece * LANES : (piece + 1) * LANES
            ]
    fetch_slab.wait()
    for piece in range(rows // LANES):
        out_ref[piece, MOST:, :] = slab_ref[:, piece * LANES : (piece + 1) * LANES]


def pick_columns(block, pivots, matrix, slab, steps=2):
    rows_dev, cols_dev = matrix.shape
    count = pivots.shape[0]
    return pl.pallas_call(
        pick_kernel,
        out_shape=jax.ShapeDtypeStruct(
            (rows_dev // LANES, MOST + slab.shape[0], LANES), jnp.float32
        ),
        in_specs=[pl.BlockSpec(memory_space=pltpu.SMEM), HBM, HBM, HBM],
        out_specs=VMEM,
        scratch_shapes=[
            pltpu.VMEM((1, count), jnp.int32),
            pltpu.VMEM((rows_dev, cols_dev), jnp.float32),
            pltpu.VMEM(slab.shape, jnp.float32),
            pltpu.SemaphoreType.DMA,
            pltpu.SemaphoreType.DMA,
            pltpu.SemaphoreType.DMA((steps,)),
        ],
        compiler_params=FETCHING,
        cost_estimate=cost(2),
        name="pick_columns",
    )(block, pivots.reshape(1, count), matrix, slab)


def sketch_kernel(gaussian_ref, matrix_ref, slab_ref, out_ref, trail_ref):
    pieces = out_ref.shape[0]
    width = matrix_ref.shape[1]
    cols = slab_ref.shape[0]
    gaussian = gaussian_ref[...]
    sketch = dot(gaussian, matrix_ref[...], 1, 0)
    for half in range(width // LANES):
        out_ref[:, 8 * half : 8 * half + 8, :] = sketch[
            :, half * LANES : (half + 1) * LANES
        ].reshape(pieces, 8, LANES)
    trail_ref[:, :cols] = dot(gaussian, slab_ref[...], 1, 1)
    packed = pack_slab(trail_ref, cols)
    at = 8 * (width // LANES)
    for piece in range(pieces):
        out_ref[piece, at : at + 2, :] = packed[2 * piece : 2 * piece + 2]
        out_ref[piece, at + 2 :, :] = jnp.zeros((6, LANES), jnp.float32)


def sketch_sums(gaussian, matrix, slab, pieces):
    return pl.pallas_call(
        sketch_kernel,
        out_shape=jax.ShapeDtypeStruct((pieces, 24, LANES), jnp.float32),
        in_specs=[VMEM] * 3,
        out_specs=VMEM,
        scratch_shapes=[pltpu.VMEM((gaussian.shape[0], LANES), jnp.float32)],
        compiler_params=PARAMS,
        cost_estimate=cost(4),
        name="sketch_sums",
    )(gaussian, matrix, slab)


def part_kernel(width, row_ref, spread_ref, sketch_ref, part_ref, send_ref, gram_ref, cross_ref):
    count = row_ref.shape[1]
    half = count // 2
    blocks = spread_ref.shape[0]
    cols = spread_ref.shape[1] - MOST
    pieces = send_ref.shape[0]
    owner_row = row_ref[...] // width
    diagonal = iota((count, count), 0) == iota((count, count), 1)
    owner = jnp.sum(jnp.where(diagonal, owner_row, 0), axis=1, keepdims=True)
    same = (owner == owner_row) & (iota((count, count), 1) < iota((count, count), 0))
    slot = jnp.sum(same.astype(jnp.int32), axis=1, keepdims=True)
    place = (iota((count, blocks * MOST), 1) == owner * MOST + slot).astype(jnp.bfloat16)
    spread = jnp.concatenate([spread_ref[b, :MOST, :] for b in range(blocks)], axis=0)
    slab = jnp.concatenate([spread_ref[b, MOST:, :] for b in range(blocks)], axis=0)
    part = hot_dot(place, spread, 1, 0)
    part_ref[...] = part
    gram_ref[...] = dot(part, part, 1, 1)
    cross_ref[0] = dot(slab, part[:half], 1, 1)
    cross_ref[1] = dot(slab, part[half:], 1, 1)
    send_ref[:, 0:16, :] = sketch_ref[:, 0:16, :]
    send_ref[:, 28:32, :] = sketch_ref[:, 16:20, :]
    for piece in range(pieces):
        low = 4 * piece
        send_ref[piece, 16:20, :] = gram_ref[low : low + 4, :half]
        send_ref[piece, 20:24, :] = gram_ref[low : low + 4, half:]
        send_ref[piece, 24:28, :] = gram_ref[half + low : half + low + 4, half:]
        send_ref[piece, 32:48, :] = cross_ref[0, pl.ds(piece, blocks, stride=cols), :]
        send_ref[piece, 48:64, :] = cross_ref[1, pl.ds(piece, blocks, stride=cols), :]


def part_products(width, pivots, spread, sketch):
    count = pivots.shape[0]
    pieces = sketch.shape[0]
    blocks = spread.shape[0]
    cols = spread.shape[1] - MOST
    return pl.pallas_call(
        functools.partial(part_kernel, width),
        out_shape=(
            jax.ShapeDtypeStruct((count, LANES), jnp.float32),
            jax.ShapeDtypeStruct((pieces, 64, LANES), jnp.float32),
        ),
        in_specs=[VMEM] * 3,
        out_specs=(VMEM,) * 2,
        scratch_shapes=[
            pltpu.VMEM((count, count), jnp.float32),
            pltpu.VMEM((2, blocks * cols, LANES), jnp.float32),
        ],
        compiler_params=PARAMS,
        cost_estimate=cost(3),
        name="part_products",
    )(pivots.reshape(1, count), spread, sketch)


def row_sums_kernel(block_ref, row_ref, got_ref, send_ref, sketch_ref, trail_ref):
    width = sketch_ref.shape[1]
    count = row_ref.shape[1]
    total = jnp.sum(got_ref[...], axis=0)
    sketch = jnp.concatenate([total[0:8], total[8:16]], axis=1)
    sketch_ref[...] = sketch
    trail_ref[...] = total[28:30]
    local_row = row_ref[...] - block_ref[0] * width
    by_column = (iota((width, count), 0) == local_row).astype(jnp.bfloat16)
    chosen = dot_hot(sketch, by_column)
    both = jnp.concatenate([chosen[:, :LANES], chosen[:, LANES:], total[16:32]], axis=0)
    for piece in range(send_ref.shape[0]):
        send_ref[piece] = both
        send_ref[piece, 28:29, :] = total[32 + piece : 33 + piece]
        send_ref[piece, 29:30, :] = total[48 + piece : 49 + piece]


def row_sums(block, pivots, got, width, pieces):
    count = pivots.shape[0]
    return pl.pallas_call(
        row_sums_kernel,
        out_shape=(
            jax.ShapeDtypeStruct((pieces, 32, LANES), jnp.float32),
            jax.ShapeDtypeStruct((8, width), jnp.float32),
            jax.ShapeDtypeStruct((2, LANES), jnp.float32),
        ),
        in_specs=[pl.BlockSpec(memory_space=pltpu.SMEM), VMEM, VMEM],
        out_specs=(VMEM,) * 3,
        compiler_params=PARAMS,
        cost_estimate=cost(1),
        name="row_sums",
    )(block, pivots.reshape(1, count), got)


def col_sums_kernel(got_ref, send_ref, gauss_ref):
    total = jnp.sum(got_ref[...], axis=0)
    gauss_ref[...] = jnp.concatenate([total[0:8], total[8:16]], axis=1)
    for piece in range(send_ref.shape[0]):
        send_ref[piece] = total[16:32]


def col_sums(got, pieces):
    return pl.pallas_call(
        col_sums_kernel,
        out_shape=(
            jax.ShapeDtypeStruct((pieces, 16, LANES), jnp.float32),
            jax.ShapeDtypeStruct((8, 2 * LANES), jnp.float32),
        ),
        in_specs=[VMEM],
        out_specs=(VMEM,) * 2,
        compiler_params=PARAMS,
        cost_estimate=cost(1),
        name="col_sums",
    )(got)


def block_inverse(block):
    n = block.shape[0]
    groups = n // 8
    sub = iota((8, 2 * n), 0)
    eye = (iota((n, n), 0) == iota((n, n), 1)).astype(jnp.float32)
    whole = jnp.concatenate([block, eye], axis=1)
    rows = [whole[8 * g : 8 * g + 8] for g in range(groups)]
    diag = [jnp.ones((8, 2 * n), jnp.float32) for _ in rows]
    for first in range(0, n, STEP):
        cols = [
            {
                g: jnp.broadcast_to(rows[g][:, j : j + 1], (8, 2 * n))
                for g in range(first // 8, groups)
            }
            for j in range(first, first + STEP)
        ]
        for t in range(STEP):
            k = first + t
            at, s = k // 8, k % 8
            col = cols[t]
            pivot = jnp.broadcast_to(col[at][s : s + 1], (8, 2 * n))
            inverse = 1.0 / pivot
            diag[at] = jnp.where(sub == s, pivot, diag[at])
            scaled = jnp.broadcast_to(rows[at][s : s + 1], (8, 2 * n)) * inverse
            for u in range(t + 1, STEP):
                other = jnp.broadcast_to(cols[u][at][s : s + 1], (8, 2 * n)) * inverse
                for g in range(at, groups):
                    cols[u][g] = cols[u][g] - col[g] * other
            for g in range(at, groups):
                factor = col[g] if g > at else jnp.where(sub > s, col[g], 0.0)
                rows[g] = rows[g] - factor * scaled
    out = jnp.concatenate([r * lax.rsqrt(d) for r, d in zip(rows, diag)], axis=0)
    return out[:, n:]


def inverse_kernel(gram_ref, out_ref, work):
    n = out_ref.shape[0]
    half = n // 2
    for piece in range(gram_ref.shape[0]):
        low = 4 * piece
        work[low : low + 4, :half] = gram_ref[piece, 0:4, :]
        work[low : low + 4, half:n] = gram_ref[piece, 4:8, :]
        work[half + low : half + low + 4, half:n] = gram_ref[piece, 8:12, :]
    work[half:, :half] = jnp.zeros((half, half), jnp.float32)
    work[:, n:] = (iota((n, n), 0) == iota((n, n), 1)).astype(jnp.float32)
    for top in range(0, n, BLOCK):
        end = top + BLOCK
        inv = block_inverse(work[top:end, top:end])
        if end == n:
            out_ref[top:end, :] = dot(inv, work[top:end, n:], 1, 0)
            break
        lo = end // LANES * LANES
        hi = -(-(n + end) // LANES) * LANES
        strip = dot(inv, work[top:end, lo:hi], 1, 0)
        done = strip[:, n - lo :]
        if hi < 2 * n:
            done = jnp.concatenate([done, jnp.zeros((BLOCK, 2 * n - hi), jnp.float32)], axis=1)
        out_ref[top:end, :] = done
        work[end:, lo:hi] -= dot(strip[:, end - lo : n - lo], strip, 0, 0)


def inverse_factor(gram, n):
    return pl.pallas_call(
        inverse_kernel,
        out_shape=jax.ShapeDtypeStruct((n, n), jnp.float32),
        in_specs=[VMEM],
        out_specs=VMEM,
        scratch_shapes=[pltpu.VMEM((n, 2 * n), jnp.float32)],
        compiler_params=PARAMS,
        cost_estimate=cost(10),
        name="inverse_factor",
    )(gram)


def finish_kernel(block_ref, inv_ref, got_ref, near_ref, far_ref, slab_ref, gauss_ref, trail_ref, coupling_ref, projected_ref, sketch_ref):
    cols = slab_ref.shape[0]
    chips = near_ref.shape[0]
    inv = inv_ref[...]
    cross = jnp.concatenate(
        [
            jnp.concatenate([got_ref[r, 12:13, :], got_ref[r, 13:14, :]], axis=1)
            for r in range(cols)
        ],
        axis=0,
    )
    coupling = dot(cross, inv, 1, 1)
    coupling_ref[...] = coupling
    weights = dot(coupling, inv, 1, 0)
    core = lax.rem(block_ref[0], 2)
    chip = lax.div(block_ref[0], 2)
    for step, hops in enumerate(HOPS):
        source = lax.rem(chip + hops, chips)
        for ref, owner in ((near_ref, 2 * source + core), (far_ref, 2 * source + 1 - core)):
            at = pl.ds(pl.multiple_of(owner * LANES, LANES), LANES)
            projected_ref[:, at] = slab_ref[:, at] - dot(weights, ref[step], 1, 0)
    per = LANES // cols
    trail = jnp.concatenate(
        [
            trail_ref[m : m + 1, p * cols : (p + 1) * cols]
            for m in range(trail_ref.shape[0])
            for p in range(per)
        ],
        axis=0,
    )
    sketch_ref[...] = trail - dot(gauss_ref[...], weights, 1, 1)


def finish(block, inv, got, near, far, slab, gauss_panel, gauss_trail):
    count = inv.shape[0]
    cols = slab.shape[0]
    return pl.pallas_call(
        finish_kernel,
        out_shape=(
            jax.ShapeDtypeStruct((cols, count), jnp.float32),
            jax.ShapeDtypeStruct(slab.shape, jnp.float32),
            jax.ShapeDtypeStruct((gauss_panel.shape[0], cols), jnp.float32),
        ),
        in_specs=[pl.BlockSpec(memory_space=pltpu.SMEM)] + [VMEM] * 7,
        out_specs=(VMEM,) * 3,
        compiler_params=PARAMS,
        cost_estimate=cost(3),
        name="finish",
    )(block, inv, got, near, far, slab, gauss_panel, gauss_trail)


def exchange(pieces, axis):
    return lax.all_to_all(pieces, axis, 0, 0, tiled=True)


def pass_on(value, chips):
    n = lax.axis_size("cols")
    return lax.ppermute(value, "cols", [(i, (i + 2 * chips) % n) for i in range(n)])


def swap_cores(value):
    n = lax.axis_size("cols")
    return lax.ppermute(value, "cols", [(i, i ^ 1) for i in range(n)])


def shards(matrix, gaussian, pivots, trailing):
    rows_dev, cols_dev = matrix.shape
    count = pivots.shape[0]
    n_rows = lax.axis_size("rows")
    n_cols = lax.axis_size("cols")
    block = lax.axis_index("cols").reshape(1)
    slab = trailing.T

    mine = pick_columns(block, pivots, matrix, slab)
    spread = exchange(mine, "cols")
    late_gaussian, mine = lax.optimization_barrier((gaussian, mine))
    sketch_part = sketch_sums(late_gaussian, matrix, slab, n_rows)
    spread, sketch_part = lax.optimization_barrier((spread, sketch_part))
    part, send = part_products(cols_dev, pivots, spread, sketch_part)

    got = exchange(send, "rows")
    part, _ = lax.optimization_barrier((part, send))
    up, down = [part], [part]
    for _ in range(2):
        up.append(pass_on(up[-1], 1))
        down.append(pass_on(down[-1], -1))
    opposite = pass_on(part, 4)
    got, up[2], down[2] = lax.optimization_barrier((got, up[2], down[2]))
    send, sketch, gauss_trail = row_sums(block, pivots, got, cols_dev, n_cols)
    got = exchange(send, "cols")
    up.append(pass_on(up[2], 1))
    down.append(pass_on(down[2], -1))
    send, gauss_panel = col_sums(got, n_rows)
    got = exchange(send, "rows")
    near = jnp.stack(up + [opposite] + down[1:])
    near, _ = lax.optimization_barrier((near, send))
    far = swap_cores(near)
    inv = inverse_factor(got, count)
    coupling, projected, trailing_sketch = finish(
        block, inv, got, near, far, slab, gauss_panel, gauss_trail
    )
    return (sketch, coupling.T, projected.T, trailing_sketch)


def solution(mesh):
    placed = (P("rows", "cols"), P(None, "rows"), P(), P("rows", "cols"))
    return jax.shard_map(
        shards,
        mesh=mesh,
        in_specs=placed,
        out_specs=(P("rows", "cols"), P(None, "cols"), P("rows", "cols"), P("rows", "cols")),
        check_vma=False,
    )
```

```python
import functools
import jax
import jax.numpy as jnp
from jax import lax
from jax.experimental import pallas as pl
from jax.experimental.pallas import tpu as pltpu
from jax.sharding import PartitionSpec as P

MOST = 64
BLOCK = 64
STEP = 16
LANES = 128
VMEM = pl.BlockSpec(memory_space=pltpu.VMEM)
HBM = pl.BlockSpec(memory_space=pltpu.HBM)
PARAMS = pltpu.CompilerParams(vmem_limit_bytes=48 * 1024 * 1024)
FETCHING = pltpu.CompilerParams(vmem_limit_bytes=60 * 1024 * 1024)


def product(left, right):
    return jnp.dot(left, right, precision=lax.Precision.HIGHEST, preferred_element_type=jnp.float32)


def dot(left, right, left_dim, right_dim):
    return lax.dot_general(
        left,
        right,
        (((left_dim,), (right_dim,)), ((), ())),
        precision=lax.Precision.HIGHEST,
        preferred_element_type=jnp.float32,
    )


def hot_dot(hot, values, hot_dim, value_dim):
    high = values.astype(jnp.bfloat16)
    rest = values - high.astype(jnp.float32)
    middle = rest.astype(jnp.bfloat16)
    low = (rest - middle.astype(jnp.float32)).astype(jnp.bfloat16)
    dims = (((hot_dim,), (value_dim,)), ((), ()))
    parts = [
        lax.dot_general(hot, piece, dims, preferred_element_type=jnp.float32)
        for piece in (high, middle, low)
    ]
    return parts[0] + parts[1] + parts[2]


def dot_hot(values, hot):
    high = values.astype(jnp.bfloat16)
    rest = values - high.astype(jnp.float32)
    middle = rest.astype(jnp.bfloat16)
    low = (rest - middle.astype(jnp.float32)).astype(jnp.bfloat16)
    parts = [
        jnp.dot(piece, hot, preferred_element_type=jnp.float32) for piece in (high, middle, low)
    ]
    return parts[0] + parts[1] + parts[2]


def cost(micros):
    return pl.CostEstimate(flops=int(micros * 1e9), bytes_accessed=0, transcendentals=0)


def iota(shape, dim):
    return lax.broadcasted_iota(jnp.int32, shape, dim)


def pack_slab(ref, cols):
    per = LANES // cols
    rows = ref.shape[0] // per
    return jnp.concatenate(
        [ref[pl.ds(p, rows, stride=per), :][:, :cols] for p in range(per)], axis=1
    )


def pick_kernel(block_ref, row_hbm, matrix_hbm, slab_hbm, out_ref, row_ref, matrix_ref, slab_ref, row_sem, slab_sem, sems):
    steps = sems.shape[0]
    rows, width = matrix_ref.shape
    count = row_ref.shape[1]
    chunk = rows // steps
    fetch_row = pltpu.make_async_copy(row_hbm, row_ref, row_sem)
    fetch_row.start()
    fetches = []
    for i in range(steps):
        at = pl.ds(i * chunk, chunk)
        fetch = pltpu.make_async_copy(matrix_hbm.at[at, :], matrix_ref.at[at, :], sems.at[i])
        fetch.start()
        fetches.append(fetch)
    fetch_slab = pltpu.make_async_copy(slab_hbm, slab_ref, slab_sem)
    fetch_slab.start()
    fetch_row.wait()
    row = row_ref[...]
    owner_row = row // width
    diagonal = iota((count, count), 0) == iota((count, count), 1)
    owner_column = jnp.sum(jnp.where(diagonal, owner_row, 0), axis=1, keepdims=True)
    same = (owner_column == owner_row) & (iota((count, count), 0) < iota((count, count), 1))
    slot_row = jnp.sum(same.astype(jnp.int32), axis=0, keepdims=True)
    local_row = row - block_ref[0] * width
    by_slot = (iota((MOST, count), 0) == slot_row).astype(jnp.bfloat16)
    by_column = (iota((width, count), 0) == local_row).astype(jnp.bfloat16)
    pick = lax.dot_general(
        by_slot, by_column, (((1,), (1,)), ((), ())), preferred_element_type=jnp.float32
    ).astype(jnp.bfloat16)
    for i in range(steps):
        fetches[i].wait()
        got = hot_dot(pick, matrix_ref[i * chunk : (i + 1) * chunk, :], 1, 1)
        for piece in range(chunk // LANES):
            out_ref[i * (chunk // LANES) + piece, :MOST, :] = got[
                :, piece * LANES : (piece + 1) * LANES
            ]
    fetch_slab.wait()
    for piece in range(rows // LANES):
        out_ref[piece, MOST:, :] = slab_ref[:, piece * LANES : (piece + 1) * LANES]


def pick_columns(block, pivots, matrix, slab, steps=2):
    rows_dev, cols_dev = matrix.shape
    count = pivots.shape[0]
    return pl.pallas_call(
        pick_kernel,
        out_shape=jax.ShapeDtypeStruct(
            (rows_dev // LANES, MOST + slab.shape[0], LANES), jnp.float32
        ),
        in_specs=[pl.BlockSpec(memory_space=pltpu.SMEM), HBM, HBM, HBM],
        out_specs=VMEM,
        scratch_shapes=[
            pltpu.VMEM((1, count), jnp.int32),
            pltpu.VMEM((rows_dev, cols_dev), jnp.float32),
            pltpu.VMEM(slab.shape, jnp.float32),
            pltpu.SemaphoreType.DMA,
            pltpu.SemaphoreType.DMA,
            pltpu.SemaphoreType.DMA((steps,)),
        ],
        compiler_params=FETCHING,
        cost_estimate=cost(2),
        name="pick_columns",
    )(block, pivots.reshape(1, count), matrix, slab)


def sketch_kernel(gaussian_ref, matrix_ref, slab_ref, out_ref, trail_ref):
    pieces = out_ref.shape[0]
    width = matrix_ref.shape[1]
    cols = slab_ref.shape[0]
    gaussian = gaussian_ref[...]
    sketch = dot(gaussian, matrix_ref[...], 1, 0)
    for half in range(width // LANES):
        out_ref[:, 8 * half : 8 * half + 8, :] = sketch[
            :, half * LANES : (half + 1) * LANES
        ].reshape(pieces, 8, LANES)
    trail_ref[:, :cols] = dot(gaussian, slab_ref[...], 1, 1)
    packed = pack_slab(trail_ref, cols)
    at = 8 * (width // LANES)
    for piece in range(pieces):
        out_ref[piece, at : at + 2, :] = packed[2 * piece : 2 * piece + 2]
        out_ref[piece, at + 2 :, :] = jnp.zeros((6, LANES), jnp.float32)


def sketch_sums(gaussian, matrix, slab, pieces):
    return pl.pallas_call(
        sketch_kernel,
        out_shape=jax.ShapeDtypeStruct((pieces, 24, LANES), jnp.float32),
        in_specs=[VMEM] * 3,
        out_specs=VMEM,
        scratch_shapes=[pltpu.VMEM((gaussian.shape[0], LANES), jnp.float32)],
        compiler_params=PARAMS,
        cost_estimate=cost(4),
        name="sketch_sums",
    )(gaussian, matrix, slab)


def part_kernel(width, row_ref, spread_ref, sketch_ref, part_ref, send_ref, gram_ref, cross_ref):
    count = row_ref.shape[1]
    half = count // 2
    blocks = spread_ref.shape[0]
    cols = spread_ref.shape[1] - MOST
    pieces = send_ref.shape[0]
    owner_row = row_ref[...] // width
    diagonal = iota((count, count), 0) == iota((count, count), 1)
    owner = jnp.sum(jnp.where(diagonal, owner_row, 0), axis=1, keepdims=True)
    same = (owner == owner_row) & (iota((count, count), 1) < iota((count, count), 0))
    slot = jnp.sum(same.astype(jnp.int32), axis=1, keepdims=True)
    place = (iota((count, blocks * MOST), 1) == owner * MOST + slot).astype(jnp.bfloat16)
    spread = jnp.concatenate([spread_ref[b, :MOST, :] for b in range(blocks)], axis=0)
    slab = jnp.concatenate([spread_ref[b, MOST:, :] for b in range(blocks)], axis=0)
    part = hot_dot(place, spread, 1, 0)
    part_ref[...] = part
    gram_ref[...] = dot(part, part, 1, 1)
    cross_ref[0] = dot(slab, part[:half], 1, 1)
    cross_ref[1] = dot(slab, part[half:], 1, 1)
    send_ref[:, 0:16, :] = sketch_ref[:, 0:16, :]
    send_ref[:, 28:32, :] = sketch_ref[:, 16:20, :]
    for piece in range(pieces):
        low = 4 * piece
        send_ref[piece, 16:20, :] = gram_ref[low : low + 4, :half]
        send_ref[piece, 20:24, :] = gram_ref[low : low + 4, half:]
        send_ref[piece, 24:28, :] = gram_ref[half + low : half + low + 4, half:]
        send_ref[piece, 32:48, :] = cross_ref[0, pl.ds(piece, blocks, stride=cols), :]
        send_ref[piece, 48:64, :] = cross_ref[1, pl.ds(piece, blocks, stride=cols), :]


def part_products(width, pivots, spread, sketch):
    count = pivots.shape[0]
    pieces = sketch.shape[0]
    blocks = spread.shape[0]
    cols = spread.shape[1] - MOST
    return pl.pallas_call(
        functools.partial(part_kernel, width),
        out_shape=(
            jax.ShapeDtypeStruct((count, LANES), jnp.float32),
            jax.ShapeDtypeStruct((pieces, 64, LANES), jnp.float32),
        ),
        in_specs=[VMEM] * 3,
        out_specs=(VMEM,) * 2,
        scratch_shapes=[
            pltpu.VMEM((count, count), jnp.float32),
            pltpu.VMEM((2, blocks * cols, LANES), jnp.float32),
        ],
        compiler_params=PARAMS,
        cost_estimate=cost(3),
        name="part_products",
    )(pivots.reshape(1, count), spread, sketch)


def row_sums_kernel(block_ref, row_ref, got_ref, send_ref, sketch_ref, trail_ref):
    width = sketch_ref.shape[1]
    count = row_ref.shape[1]
    total = jnp.sum(got_ref[...], axis=0)
    sketch = jnp.concatenate([total[0:8], total[8:16]], axis=1)
    sketch_ref[...] = sketch
    trail_ref[...] = total[28:30]
    local_row = row_ref[...] - block_ref[0] * width
    by_column = (iota((width, count), 0) == local_row).astype(jnp.bfloat16)
    chosen = dot_hot(sketch, by_column)
    both = jnp.concatenate([chosen[:, :LANES], chosen[:, LANES:], total[16:32]], axis=0)
    for piece in range(send_ref.shape[0]):
        send_ref[piece] = both
        send_ref[piece, 28:29, :] = total[32 + piece : 33 + piece]
        send_ref[piece, 29:30, :] = total[48 + piece : 49 + piece]


def row_sums(block, pivots, got, width, pieces):
    count = pivots.shape[0]
    return pl.pallas_call(
        row_sums_kernel,
        out_shape=(
            jax.ShapeDtypeStruct((pieces, 32, LANES), jnp.float32),
            jax.ShapeDtypeStruct((8, width), jnp.float32),
            jax.ShapeDtypeStruct((2, LANES), jnp.float32),
        ),
        in_specs=[pl.BlockSpec(memory_space=pltpu.SMEM), VMEM, VMEM],
        out_specs=(VMEM,) * 3,
        compiler_params=PARAMS,
        cost_estimate=cost(1),
        name="row_sums",
    )(block, pivots.reshape(1, count), got)


def col_sums_kernel(got_ref, send_ref, gauss_ref):
    total = jnp.sum(got_ref[...], axis=0)
    gauss_ref[...] = jnp.concatenate([total[0:8], total[8:16]], axis=1)
    for piece in range(send_ref.shape[0]):
        send_ref[piece] = total[16:32]


def col_sums(got, pieces):
    return pl.pallas_call(
        col_sums_kernel,
        out_shape=(
            jax.ShapeDtypeStruct((pieces, 16, LANES), jnp.float32),
            jax.ShapeDtypeStruct((8, 2 * LANES), jnp.float32),
        ),
        in_specs=[VMEM],
        out_specs=(VMEM,) * 2,
        compiler_params=PARAMS,
        cost_estimate=cost(1),
        name="col_sums",
    )(got)


def block_inverse(block):
    n = block.shape[0]
    groups = n // 8
    sub = iota((8, 2 * n), 0)
    eye = (iota((n, n), 0) == iota((n, n), 1)).astype(jnp.float32)
    whole = jnp.concatenate([block, eye], axis=1)
    rows = [whole[8 * g : 8 * g + 8] for g in range(groups)]
    diag = [jnp.ones((8, 2 * n), jnp.float32) for _ in rows]
    for first in range(0, n, STEP):
        cols = [
            {
                g: jnp.broadcast_to(rows[g][:, j : j + 1], (8, 2 * n))
                for g in range(first // 8, groups)
            }
            for j in range(first, first + STEP)
        ]
        for t in range(STEP):
            k = first + t
            at, s = k // 8, k % 8
            col = cols[t]
            pivot = jnp.broadcast_to(col[at][s : s + 1], (8, 2 * n))
            inverse = 1.0 / pivot
            diag[at] = jnp.where(sub == s, pivot, diag[at])
            scaled = jnp.broadcast_to(rows[at][s : s + 1], (8, 2 * n)) * inverse
            for u in range(t + 1, STEP):
                other = jnp.broadcast_to(cols[u][at][s : s + 1], (8, 2 * n)) * inverse
                for g in range(at, groups):
                    cols[u][g] = cols[u][g] - col[g] * other
            for g in range(at, groups):
                factor = col[g] if g > at else jnp.where(sub > s, col[g], 0.0)
                rows[g] = rows[g] - factor * scaled
    out = jnp.concatenate([r * lax.rsqrt(d) for r, d in zip(rows, diag)], axis=0)
    return out[:, n:]


def inverse_kernel(gram_ref, out_ref, work):
    n = out_ref.shape[0]
    half = n // 2
    for piece in range(gram_ref.shape[0]):
        low = 4 * piece
        work[low : low + 4, :half] = gram_ref[piece, 0:4, :]
        work[low : low + 4, half:n] = gram_ref[piece, 4:8, :]
        work[half + low : half + low + 4, half:n] = gram_ref[piece, 8:12, :]
    work[half:, :half] = jnp.zeros((half, half), jnp.float32)
    work[:, n:] = (iota((n, n), 0) == iota((n, n), 1)).astype(jnp.float32)
    for top in range(0, n, BLOCK):
        end = top + BLOCK
        inv = block_inverse(work[top:end, top:end])
        if end == n:
            out_ref[top:end, :] = dot(inv, work[top:end, n:], 1, 0)
            break
        lo = end // LANES * LANES
        hi = -(-(n + end) // LANES) * LANES
        strip = dot(inv, work[top:end, lo:hi], 1, 0)
        done = strip[:, n - lo :]
        if hi < 2 * n:
            done = jnp.concatenate([done, jnp.zeros((BLOCK, 2 * n - hi), jnp.float32)], axis=1)
        out_ref[top:end, :] = done
        work[end:, lo:hi] -= dot(strip[:, end - lo : n - lo], strip, 0, 0)


def inverse_factor(gram, n):
    return pl.pallas_call(
        inverse_kernel,
        out_shape=jax.ShapeDtypeStruct((n, n), jnp.float32),
        in_specs=[VMEM],
        out_specs=VMEM,
        scratch_shapes=[pltpu.VMEM((n, 2 * n), jnp.float32)],
        compiler_params=PARAMS,
        cost_estimate=cost(10),
        name="inverse_factor",
    )(gram)


def finish_kernel(block_ref, inv_ref, got_ref, own_ref, other_ref, one_ref, two_ref, three_ref, four_ref, far_ref, slab_ref, gauss_ref, trail_ref, coupling_ref, projected_ref, sketch_ref):
    cols = slab_ref.shape[0]
    inv = inv_ref[...]
    cross = jnp.concatenate(
        [
            jnp.concatenate([got_ref[r, 12:13, :], got_ref[r, 13:14, :]], axis=1)
            for r in range(cols)
        ],
        axis=0,
    )
    coupling = dot(cross, inv, 1, 1)
    coupling_ref[...] = coupling
    weights = dot(coupling, inv, 1, 0)
    chips = slab_ref.shape[1] // (2 * LANES)
    core = lax.rem(block_ref[0], 2)
    chip = lax.div(block_ref[0], 2)
    toward = 2 * core - 1
    blocks = [(own_ref, None, 0, core), (other_ref, None, 0, 1 - core)]
    for steps, ref in ((1, one_ref), (2, two_ref), (3, three_ref), (4, four_ref)):
        blocks += [(ref, 0, steps * toward, core), (ref, 1, steps * toward, 1 - core)]
    for steps in (1, 2, 3):
        blocks += [
            (far_ref, 2 * steps - 2, -steps * toward, 1 - core),
            (far_ref, 2 * steps - 1, -steps * toward, core),
        ]
    for ref, index, hops, owner_core in blocks:
        owner = 2 * lax.rem(chip + hops + chips, chips) + owner_core
        at = pl.ds(pl.multiple_of(owner * LANES, LANES), LANES)
        value = ref[...] if index is None else ref[index]
        projected_ref[:, at] = slab_ref[:, at] - dot(weights, value, 1, 0)
    per = LANES // cols
    trail = jnp.concatenate(
        [
            trail_ref[m : m + 1, p * cols : (p + 1) * cols]
            for m in range(trail_ref.shape[0])
            for p in range(per)
        ],
        axis=0,
    )
    sketch_ref[...] = trail - dot(gauss_ref[...], weights, 1, 1)


def finish(block, inv, got, panel, slab, gauss_panel, gauss_trail):
    count = inv.shape[0]
    cols = slab.shape[0]
    return pl.pallas_call(
        finish_kernel,
        out_shape=(
            jax.ShapeDtypeStruct((cols, count), jnp.float32),
            jax.ShapeDtypeStruct(slab.shape, jnp.float32),
            jax.ShapeDtypeStruct((gauss_panel.shape[0], cols), jnp.float32),
        ),
        in_specs=[pl.BlockSpec(memory_space=pltpu.SMEM)] + [VMEM] * (5 + len(panel)),
        out_specs=(VMEM,) * 3,
        compiler_params=PARAMS,
        cost_estimate=cost(3),
        name="finish",
    )(block, inv, got, *panel, slab, gauss_panel, gauss_trail)


def exchange(pieces, axis):
    return lax.all_to_all(pieces, axis, 0, 0, tiled=True)


def pass_round(value):
    n = lax.axis_size("cols")
    return lax.ppermute(value, "cols", [(i, (i + (2 if i % 2 == 0 else -2)) % n) for i in range(n)])


def swap_cores(value):
    n = lax.axis_size("cols")
    return lax.ppermute(value, "cols", [(i, i ^ 1) for i in range(n)])


def shards(matrix, gaussian, pivots, trailing):
    rows_dev, cols_dev = matrix.shape
    count = pivots.shape[0]
    n_rows = lax.axis_size("rows")
    n_cols = lax.axis_size("cols")
    block = lax.axis_index("cols").reshape(1)
    slab = trailing.T

    mine = pick_columns(block, pivots, matrix, slab)
    spread = exchange(mine, "cols")
    late_gaussian, mine = lax.optimization_barrier((gaussian, mine))
    sketch_part = sketch_sums(late_gaussian, matrix, slab, n_rows)
    spread, sketch_part = lax.optimization_barrier((spread, sketch_part))
    part, send = part_products(cols_dev, pivots, spread, sketch_part)

    got = exchange(send, "rows")
    part, _ = lax.optimization_barrier((part, send))
    other = swap_cores(part)
    one = pass_round(jnp.stack([part, other]))
    two = pass_round(one)
    got, two = lax.optimization_barrier((got, two))
    send, sketch, gauss_trail = row_sums(block, pivots, got, cols_dev, n_cols)
    got = exchange(send, "cols")
    held, _ = lax.optimization_barrier((two, send))
    three = pass_round(held)
    got, three = lax.optimization_barrier((got, three))
    send, gauss_panel = col_sums(got, n_rows)
    got = exchange(send, "rows")
    last, _ = lax.optimization_barrier((three, send))
    four = pass_round(last)
    held, _ = lax.optimization_barrier((jnp.concatenate([one, two, last]), send))
    far = swap_cores(held)
    inv = inverse_factor(got, count)
    coupling, projected, trailing_sketch = finish(
        block,
        inv,
        got,
        (part, other, one, two, three, four, far),
        slab,
        gauss_panel,
        gauss_trail,
    )
    return (sketch, coupling.T, projected.T, trailing_sketch)


def solution(mesh):
    placed = (P("rows", "cols"), P(None, "rows"), P(), P("rows", "cols"))
    return jax.shard_map(
        shards,
        mesh=mesh,
        in_specs=placed,
        out_specs=(P("rows", "cols"), P(None, "cols"), P("rows", "cols"), P("rows", "cols")),
        check_vma=False,
    )
```

```python
import functools
import jax
import jax.numpy as jnp
from jax import lax
from jax.experimental import pallas as pl
from jax.experimental.pallas import tpu as pltpu
from jax.sharding import PartitionSpec as P

MOST = 64
BLOCK = 64
STEP = 16
LANES = 128
VMEM = pl.BlockSpec(memory_space=pltpu.VMEM)
HBM = pl.BlockSpec(memory_space=pltpu.HBM)
PARAMS = pltpu.CompilerParams(vmem_limit_bytes=48 * 1024 * 1024)
FETCHING = pltpu.CompilerParams(vmem_limit_bytes=60 * 1024 * 1024)


def product(left, right):
    return jnp.dot(left, right, precision=lax.Precision.HIGHEST, preferred_element_type=jnp.float32)


def dot(left, right, left_dim, right_dim):
    return lax.dot_general(
        left,
        right,
        (((left_dim,), (right_dim,)), ((), ())),
        precision=lax.Precision.HIGHEST,
        preferred_element_type=jnp.float32,
    )


def hot_dot(hot, values, hot_dim, value_dim):
    high = values.astype(jnp.bfloat16)
    rest = values - high.astype(jnp.float32)
    middle = rest.astype(jnp.bfloat16)
    low = (rest - middle.astype(jnp.float32)).astype(jnp.bfloat16)
    dims = (((hot_dim,), (value_dim,)), ((), ()))
    parts = [
        lax.dot_general(hot, piece, dims, preferred_element_type=jnp.float32)
        for piece in (high, middle, low)
    ]
    return parts[0] + parts[1] + parts[2]


def dot_hot(values, hot):
    high = values.astype(jnp.bfloat16)
    rest = values - high.astype(jnp.float32)
    middle = rest.astype(jnp.bfloat16)
    low = (rest - middle.astype(jnp.float32)).astype(jnp.bfloat16)
    parts = [
        jnp.dot(piece, hot, preferred_element_type=jnp.float32) for piece in (high, middle, low)
    ]
    return parts[0] + parts[1] + parts[2]


def cost(micros):
    return pl.CostEstimate(flops=int(micros * 1e9), bytes_accessed=0, transcendentals=0)


def iota(shape, dim):
    return lax.broadcasted_iota(jnp.int32, shape, dim)


def pack_slab(ref, cols):
    per = LANES // cols
    rows = ref.shape[0] // per
    return jnp.concatenate(
        [ref[pl.ds(p, rows, stride=per), :][:, :cols] for p in range(per)], axis=1
    )


def pick_kernel(block_ref, row_hbm, matrix_hbm, slab_hbm, out_ref, row_ref, matrix_ref, slab_ref, row_sem, slab_sem, sems):
    steps = sems.shape[0]
    rows, width = matrix_ref.shape
    count = row_ref.shape[1]
    chunk = rows // steps
    fetch_row = pltpu.make_async_copy(row_hbm, row_ref, row_sem)
    fetch_row.start()
    fetches = []
    for i in range(steps):
        at = pl.ds(i * chunk, chunk)
        fetch = pltpu.make_async_copy(matrix_hbm.at[at, :], matrix_ref.at[at, :], sems.at[i])
        fetch.start()
        fetches.append(fetch)
    fetch_slab = pltpu.make_async_copy(slab_hbm, slab_ref, slab_sem)
    fetch_slab.start()
    fetch_row.wait()
    row = row_ref[...]
    owner_row = row // width
    diagonal = iota((count, count), 0) == iota((count, count), 1)
    owner_column = jnp.sum(jnp.where(diagonal, owner_row, 0), axis=1, keepdims=True)
    same = (owner_column == owner_row) & (iota((count, count), 0) < iota((count, count), 1))
    slot_row = jnp.sum(same.astype(jnp.int32), axis=0, keepdims=True)
    local_row = row - block_ref[0] * width
    by_slot = (iota((MOST, count), 0) == slot_row).astype(jnp.bfloat16)
    by_column = (iota((width, count), 0) == local_row).astype(jnp.bfloat16)
    pick = lax.dot_general(
        by_slot, by_column, (((1,), (1,)), ((), ())), preferred_element_type=jnp.float32
    ).astype(jnp.bfloat16)
    for i in range(steps):
        fetches[i].wait()
        got = hot_dot(pick, matrix_ref[i * chunk : (i + 1) * chunk, :], 1, 1)
        for piece in range(chunk // LANES):
            out_ref[i * (chunk // LANES) + piece, :MOST, :] = got[
                :, piece * LANES : (piece + 1) * LANES
            ]
    fetch_slab.wait()
    for piece in range(rows // LANES):
        out_ref[piece, MOST:, :] = slab_ref[:, piece * LANES : (piece + 1) * LANES]


def pick_columns(block, pivots, matrix, slab, steps=2):
    rows_dev, cols_dev = matrix.shape
    count = pivots.shape[0]
    return pl.pallas_call(
        pick_kernel,
        out_shape=jax.ShapeDtypeStruct(
            (rows_dev // LANES, MOST + slab.shape[0], LANES), jnp.float32
        ),
        in_specs=[pl.BlockSpec(memory_space=pltpu.SMEM), HBM, HBM, HBM],
        out_specs=VMEM,
        scratch_shapes=[
            pltpu.VMEM((1, count), jnp.int32),
            pltpu.VMEM((rows_dev, cols_dev), jnp.float32),
            pltpu.VMEM(slab.shape, jnp.float32),
            pltpu.SemaphoreType.DMA,
            pltpu.SemaphoreType.DMA,
            pltpu.SemaphoreType.DMA((steps,)),
        ],
        compiler_params=FETCHING,
        cost_estimate=cost(2),
        name="pick_columns",
    )(block, pivots.reshape(1, count), matrix, slab)


def sketch_kernel(gaussian_ref, matrix_ref, slab_ref, out_ref, trail_ref):
    pieces = out_ref.shape[0]
    width = matrix_ref.shape[1]
    cols = slab_ref.shape[0]
    gaussian = gaussian_ref[...]
    sketch = dot(gaussian, matrix_ref[...], 1, 0)
    for half in range(width // LANES):
        out_ref[:, 8 * half : 8 * half + 8, :] = sketch[
            :, half * LANES : (half + 1) * LANES
        ].reshape(pieces, 8, LANES)
    trail_ref[:, :cols] = dot(gaussian, slab_ref[...], 1, 1)
    packed = pack_slab(trail_ref, cols)
    at = 8 * (width // LANES)
    for piece in range(pieces):
        out_ref[piece, at : at + 2, :] = packed[2 * piece : 2 * piece + 2]
        out_ref[piece, at + 2 :, :] = jnp.zeros((6, LANES), jnp.float32)


def sketch_sums(gaussian, matrix, slab, pieces):
    return pl.pallas_call(
        sketch_kernel,
        out_shape=jax.ShapeDtypeStruct((pieces, 24, LANES), jnp.float32),
        in_specs=[VMEM] * 3,
        out_specs=VMEM,
        scratch_shapes=[pltpu.VMEM((gaussian.shape[0], LANES), jnp.float32)],
        compiler_params=PARAMS,
        cost_estimate=cost(4),
        name="sketch_sums",
    )(gaussian, matrix, slab)


def part_kernel(width, row_ref, spread_ref, sketch_ref, part_ref, send_ref, gram_ref, cross_ref):
    count = row_ref.shape[1]
    half = count // 2
    blocks = spread_ref.shape[0]
    cols = spread_ref.shape[1] - MOST
    pieces = send_ref.shape[0]
    owner_row = row_ref[...] // width
    diagonal = iota((count, count), 0) == iota((count, count), 1)
    owner = jnp.sum(jnp.where(diagonal, owner_row, 0), axis=1, keepdims=True)
    same = (owner == owner_row) & (iota((count, count), 1) < iota((count, count), 0))
    slot = jnp.sum(same.astype(jnp.int32), axis=1, keepdims=True)
    place = (iota((count, blocks * MOST), 1) == owner * MOST + slot).astype(jnp.bfloat16)
    spread = jnp.concatenate([spread_ref[b, :MOST, :] for b in range(blocks)], axis=0)
    slab = jnp.concatenate([spread_ref[b, MOST:, :] for b in range(blocks)], axis=0)
    part = hot_dot(place, spread, 1, 0)
    part_ref[...] = part
    gram_ref[...] = dot(part, part, 1, 1)
    cross = dot(slab, part, 1, 1)
    cross_ref[0] = cross[:, :half]
    cross_ref[1] = cross[:, half:]
    send_ref[:, 0:16, :] = sketch_ref[:, 0:16, :]
    send_ref[:, 28:32, :] = sketch_ref[:, 16:20, :]
    for piece in range(pieces):
        low = 4 * piece
        send_ref[piece, 16:20, :] = gram_ref[low : low + 4, :half]
        send_ref[piece, 20:24, :] = gram_ref[low : low + 4, half:]
        send_ref[piece, 24:28, :] = gram_ref[half + low : half + low + 4, half:]
        send_ref[piece, 32:48, :] = cross_ref[0, pl.ds(piece, blocks, stride=cols), :]
        send_ref[piece, 48:64, :] = cross_ref[1, pl.ds(piece, blocks, stride=cols), :]


def part_products(width, pivots, spread, sketch):
    count = pivots.shape[0]
    pieces = sketch.shape[0]
    blocks = spread.shape[0]
    cols = spread.shape[1] - MOST
    return pl.pallas_call(
        functools.partial(part_kernel, width),
        out_shape=(
            jax.ShapeDtypeStruct((count, LANES), jnp.float32),
            jax.ShapeDtypeStruct((pieces, 64, LANES), jnp.float32),
        ),
        in_specs=[VMEM] * 3,
        out_specs=(VMEM,) * 2,
        scratch_shapes=[
            pltpu.VMEM((count, count), jnp.float32),
            pltpu.VMEM((2, blocks * cols, LANES), jnp.float32),
        ],
        compiler_params=PARAMS,
        cost_estimate=cost(3),
        name="part_products",
    )(pivots.reshape(1, count), spread, sketch)


def row_sums_kernel(block_ref, row_ref, got_ref, send_ref, sketch_ref, trail_ref):
    width = sketch_ref.shape[1]
    count = row_ref.shape[1]
    total = jnp.sum(got_ref[...], axis=0)
    sketch = jnp.concatenate([total[0:8], total[8:16]], axis=1)
    sketch_ref[...] = sketch
    trail_ref[...] = total[28:30]
    local_row = row_ref[...] - block_ref[0] * width
    by_column = (iota((width, count), 0) == local_row).astype(jnp.bfloat16)
    chosen = dot_hot(sketch, by_column)
    both = jnp.concatenate([chosen[:, :LANES], chosen[:, LANES:], total[16:32]], axis=0)
    for piece in range(send_ref.shape[0]):
        send_ref[piece] = both
        send_ref[piece, 28:29, :] = total[32 + piece : 33 + piece]
        send_ref[piece, 29:30, :] = total[48 + piece : 49 + piece]


def row_sums(block, pivots, got, width, pieces):
    count = pivots.shape[0]
    return pl.pallas_call(
        row_sums_kernel,
        out_shape=(
            jax.ShapeDtypeStruct((pieces, 32, LANES), jnp.float32),
            jax.ShapeDtypeStruct((8, width), jnp.float32),
            jax.ShapeDtypeStruct((2, LANES), jnp.float32),
        ),
        in_specs=[pl.BlockSpec(memory_space=pltpu.SMEM), VMEM, VMEM],
        out_specs=(VMEM,) * 3,
        compiler_params=PARAMS,
        cost_estimate=cost(1),
        name="row_sums",
    )(block, pivots.reshape(1, count), got)


def col_sums_kernel(got_ref, send_ref, gauss_ref):
    total = jnp.sum(got_ref[...], axis=0)
    gauss_ref[...] = jnp.concatenate([total[0:8], total[8:16]], axis=1)
    for piece in range(send_ref.shape[0]):
        send_ref[piece] = total[16:32]


def col_sums(got, pieces):
    return pl.pallas_call(
        col_sums_kernel,
        out_shape=(
            jax.ShapeDtypeStruct((pieces, 16, LANES), jnp.float32),
            jax.ShapeDtypeStruct((8, 2 * LANES), jnp.float32),
        ),
        in_specs=[VMEM],
        out_specs=(VMEM,) * 2,
        compiler_params=PARAMS,
        cost_estimate=cost(1),
        name="col_sums",
    )(got)


def block_inverse(block):
    n = block.shape[0]
    groups = n // 8
    sub = iota((8, 2 * n), 0)
    eye = (iota((n, n), 0) == iota((n, n), 1)).astype(jnp.float32)
    whole = jnp.concatenate([block, eye], axis=1)
    rows = [whole[8 * g : 8 * g + 8] for g in range(groups)]
    diag = [jnp.ones((8, 2 * n), jnp.float32) for _ in rows]
    for first in range(0, n, STEP):
        cols = [
            {
                g: jnp.broadcast_to(rows[g][:, j : j + 1], (8, 2 * n))
                for g in range(first // 8, groups)
            }
            for j in range(first, first + STEP)
        ]
        for t in range(STEP):
            k = first + t
            at, s = k // 8, k % 8
            col = cols[t]
            pivot = jnp.broadcast_to(col[at][s : s + 1], (8, 2 * n))
            inverse = 1.0 / pivot
            diag[at] = jnp.where(sub == s, pivot, diag[at])
            scaled = jnp.broadcast_to(rows[at][s : s + 1], (8, 2 * n)) * inverse
            for u in range(t + 1, STEP):
                other = jnp.broadcast_to(cols[u][at][s : s + 1], (8, 2 * n)) * inverse
                for g in range(at, groups):
                    cols[u][g] = cols[u][g] - col[g] * other
            for g in range(at, groups):
                factor = col[g] if g > at else jnp.where(sub > s, col[g], 0.0)
                rows[g] = rows[g] - factor * scaled
    out = jnp.concatenate([r * lax.rsqrt(d) for r, d in zip(rows, diag)], axis=0)
    return out[:, n:]


def inverse_kernel(gram_ref, out_ref, work):
    n = out_ref.shape[0]
    half = n // 2
    for piece in range(gram_ref.shape[0]):
        low = 4 * piece
        work[low : low + 4, :half] = gram_ref[piece, 0:4, :]
        work[low : low + 4, half:n] = gram_ref[piece, 4:8, :]
        work[half + low : half + low + 4, half:n] = gram_ref[piece, 8:12, :]
    work[half:, :half] = jnp.zeros((half, half), jnp.float32)
    work[:, n:] = (iota((n, n), 0) == iota((n, n), 1)).astype(jnp.float32)
    for top in range(0, n, BLOCK):
        end = top + BLOCK
        inv = block_inverse(work[top:end, top:end])
        if end == n:
            out_ref[top:end, :] = dot(inv, work[top:end, n:], 1, 0)
            break
        lo = end // LANES * LANES
        hi = -(-(n + end) // LANES) * LANES
        strip = dot(inv, work[top:end, lo:hi], 1, 0)
        done = strip[:, n - lo :]
        if hi < 2 * n:
            done = jnp.concatenate([done, jnp.zeros((BLOCK, 2 * n - hi), jnp.float32)], axis=1)
        out_ref[top:end, :] = done
        work[end:, lo:hi] -= dot(strip[:, end - lo : n - lo], strip, 0, 0)


def inverse_factor(gram, n):
    return pl.pallas_call(
        inverse_kernel,
        out_shape=jax.ShapeDtypeStruct((n, n), jnp.float32),
        in_specs=[VMEM],
        out_specs=VMEM,
        scratch_shapes=[pltpu.VMEM((n, 2 * n), jnp.float32)],
        compiler_params=PARAMS,
        cost_estimate=cost(10),
        name="inverse_factor",
    )(gram)


def finish_kernel(block_ref, inv_ref, got_ref, own_ref, other_ref, one_ref, two_ref, three_ref, four_ref, far_ref, slab_ref, gauss_ref, trail_ref, coupling_ref, projected_ref, sketch_ref):
    cols = slab_ref.shape[0]
    inv = inv_ref[...]
    cross = jnp.concatenate(
        [
            jnp.concatenate([got_ref[r, 12:13, :], got_ref[r, 13:14, :]], axis=1)
            for r in range(cols)
        ],
        axis=0,
    )
    coupling = dot(cross, inv, 1, 1)
    coupling_ref[...] = coupling
    weights = dot(coupling, inv, 1, 0)
    chips = slab_ref.shape[1] // (2 * LANES)
    core = lax.rem(block_ref[0], 2)
    chip = lax.div(block_ref[0], 2)
    toward = 2 * core - 1
    pairs = [((own_ref[...], other_ref[...]), 0, core)]
    for steps, ref in ((1, one_ref), (2, two_ref), (3, three_ref), (4, four_ref)):
        pairs.append(((ref[0], ref[1]), steps * toward, core))
    for steps in (1, 2, 3):
        pairs.append(((far_ref[2 * steps - 2], far_ref[2 * steps - 1]), -steps * toward, 1 - core))
    for values, hops, first_core in pairs:
        taken = dot(weights, jnp.concatenate(values, axis=1), 1, 0)
        source = 2 * lax.rem(chip + hops + chips, chips)
        for half, owner in enumerate((source + first_core, source + 1 - first_core)):
            at = pl.ds(pl.multiple_of(owner * LANES, LANES), LANES)
            part = taken[:, half * LANES : (half + 1) * LANES]
            projected_ref[:, at] = slab_ref[:, at] - part
    per = LANES // cols
    trail = jnp.concatenate(
        [
            trail_ref[m : m + 1, p * cols : (p + 1) * cols]
            for m in range(trail_ref.shape[0])
            for p in range(per)
        ],
        axis=0,
    )
    sketch_ref[...] = trail - dot(gauss_ref[...], weights, 1, 1)


def finish(block, inv, got, panel, slab, gauss_panel, gauss_trail):
    count = inv.shape[0]
    cols = slab.shape[0]
    return pl.pallas_call(
        finish_kernel,
        out_shape=(
            jax.ShapeDtypeStruct((cols, count), jnp.float32),
            jax.ShapeDtypeStruct(slab.shape, jnp.float32),
            jax.ShapeDtypeStruct((gauss_panel.shape[0], cols), jnp.float32),
        ),
        in_specs=[pl.BlockSpec(memory_space=pltpu.SMEM)] + [VMEM] * (5 + len(panel)),
        out_specs=(VMEM,) * 3,
        compiler_params=PARAMS,
        cost_estimate=cost(3),
        name="finish",
    )(block, inv, got, *panel, slab, gauss_panel, gauss_trail)


def exchange(pieces, axis):
    return lax.all_to_all(pieces, axis, 0, 0, tiled=True)


def pass_round(value):
    n = lax.axis_size("cols")
    return lax.ppermute(value, "cols", [(i, (i + (2 if i % 2 == 0 else -2)) % n) for i in range(n)])


def swap_cores(value):
    n = lax.axis_size("cols")
    return lax.ppermute(value, "cols", [(i, i ^ 1) for i in range(n)])


def shards(matrix, gaussian, pivots, trailing):
    rows_dev, cols_dev = matrix.shape
    count = pivots.shape[0]
    n_rows = lax.axis_size("rows")
    n_cols = lax.axis_size("cols")
    block = lax.axis_index("cols").reshape(1)
    slab = trailing.T

    mine = pick_columns(block, pivots, matrix, slab)
    spread = exchange(mine, "cols")
    late_gaussian, mine = lax.optimization_barrier((gaussian, mine))
    sketch_part = sketch_sums(late_gaussian, matrix, slab, n_rows)
    spread, sketch_part = lax.optimization_barrier((spread, sketch_part))
    part, send = part_products(cols_dev, pivots, spread, sketch_part)

    got = exchange(send, "rows")
    part, _ = lax.optimization_barrier((part, send))
    other = swap_cores(part)
    one = pass_round(jnp.stack([part, other]))
    two = pass_round(one)
    got, two = lax.optimization_barrier((got, two))
    send, sketch, gauss_trail = row_sums(block, pivots, got, cols_dev, n_cols)
    got = exchange(send, "cols")
    held, _ = lax.optimization_barrier((two, send))
    three = pass_round(held)
    got, three = lax.optimization_barrier((got, three))
    send, gauss_panel = col_sums(got, n_rows)
    got = exchange(send, "rows")
    last, _ = lax.optimization_barrier((three, send))
    four = pass_round(last)
    held, _ = lax.optimization_barrier((jnp.concatenate([one, two, last]), send))
    far = swap_cores(held)
    inv = inverse_factor(got, count)
    coupling, projected, trailing_sketch = finish(
        block,
        inv,
        got,
        (part, other, one, two, three, four, far),
        slab,
        gauss_panel,
        gauss_trail,
    )
    return (sketch, coupling.T, projected.T, trailing_sketch)


def solution(mesh):
    placed = (P("rows", "cols"), P(None, "rows"), P(), P("rows", "cols"))
    return jax.shard_map(
        shards,
        mesh=mesh,
        in_specs=placed,
        out_specs=(P("rows", "cols"), P(None, "cols"), P("rows", "cols"), P("rows", "cols")),
        check_vma=False,
    )
```
